256 devices in a mesh: ctx: 64 (over z, y_lo, x), head: 4 (over y_hi, core).
Axes of the slice: x: 4, y: 4 (y_hi: 2, y_lo: 2; y = y_hi * 2 + y_lo), z: 8, core: 2. Of those that a mesh axis runs over, the one named last changes fastest.
Arguments:
- rotated_queries: bfloat16 [16384, 4096], P('ctx', 'head')
- rotated_keys: bfloat16 [16384, 512], P('ctx', 'head')
- projected_values: bfloat16 [16384, 512], P('ctx', 'head'), may hold values from -6 to 6
- doc_ids: int32 [16384], P('ctx'), may hold values from 0 to 15, never falling along the last dimension, each value on 1 to 2048 neighbouring positions
- w_out: bfloat16 [4096, 2560], P('head'), may hold values from -0.125 to 0.125
Outputs:
- mixed_out: bfloat16 [16384, 2560], P('ctx', 'head')
The draws below stay inside these ranges and needn't reach their ends.
Inputs may be any that keep to these rules, and one draw needn't show every extreme that they name: `doc_ids`: document numbers never fall along the pack; each document has at most 2048 tokens, and one has exactly 2048.
All inputs are finite; a program needn't handle non-finite values.
Results may differ from the reference program's by a relative error of at most 0.014.
Values may be sent and summed in bfloat16 or wider, within the bound.
A program may use at most 320 MiB of HBM per device.

```python
import math
import jax
import jax.numpy as jnp
import numpy as np
from jax import lax

QUERY_HEADS = 32
KEY_VALUE_HEADS = 4
HEAD_SIZE = 128
DOUT = 2560
TOKENS_PER_SHARD = 256
MAXDOC = 2048
PACK_TOKENS = 16384
DOCS = 16
N_HEAD = 4


def shared_keys(key):
    return jax.random.normal(key, (PACK_TOKENS, KEY_VALUE_HEADS, HEAD_SIZE), jnp.float32)


def draw_rotated_keys(key, part):
    shared_state = shared_keys(key)
    return shared_state.reshape(PACK_TOKENS, KEY_VALUE_HEADS * HEAD_SIZE).astype(jnp.bfloat16)


def draw_rotated_queries(key, part):
    key = jax.random.fold_in(key, 7)
    fresh = jax.random.normal(key, (PACK_TOKENS, QUERY_HEADS, HEAD_SIZE), jnp.float32)
    return fresh.reshape(PACK_TOKENS, QUERY_HEADS * HEAD_SIZE).astype(jnp.bfloat16)


def with_spikes(drawn, stream_key, source, target, blocks, factor):
    def block_of(dim):
        return (jnp.arange(drawn.shape[dim]) // (drawn.shape[dim] // blocks)).reshape((-1,) + (1,) * (drawn.ndim - 1 - dim))

    near = jax.random.permutation(stream_key, blocks)[block_of(target)]
    far = (block_of(target) + blocks // 2) % blocks
    return jnp.where((block_of(source) == near) | (block_of(source) == far), factor * drawn, drawn)


def levels(own_key, dims, shards, smallest, largest):
    level = 1.0
    for dim, parts in shards:
        steps = jax.random.uniform(jax.random.fold_in(jax.random.fold_in(own_key, 6), dim), (parts,), jnp.float32, smallest / len(shards), largest / len(shards))
        level = level * jnp.repeat(jnp.exp(steps), dims[dim] // parts).reshape((-1,) + (1,) * (len(dims) - 1 - dim))
    return level


def profile(amount, total, reach, skew):
    weights = [(1 << 20) // math.isqrt(grade ** skew) + 1 for grade in range(2, amount + 1)]
    rest, counts = total - reach - (amount - 1), [1] * (amount - 1)
    while rest > 0:
        candidates = [i for i in range(amount - 1) if counts[i] < reach]
        mass, remaining = sum([weights[i] for i in candidates]), rest
        for i in candidates:
            addition = min(reach - counts[i], max(1, remaining * weights[i] // mass), rest)
            counts[i] = counts[i] + addition
            rest = rest - addition
    return np.array([reach] + counts)


def uneven_parts(own_key, number_of, total, bound, slope):
    if number_of == 2:
        one = jax.random.randint(own_key, (), max(1, total - bound), min(bound, total - 1) + 1)
        return jnp.stack([one, total - one])
    lengths = jnp.asarray(profile(number_of, total, bound, slope), jnp.int32)
    twos = (number_of - 1) // 2
    source_of, sink = lengths[1:1 + 2 * twos:2], lengths[2:2 + 2 * twos:2]
    room = jnp.minimum(source_of - 1, bound - sink)
    moved = jax.random.randint(jax.random.fold_in(own_key, 1), (twos,), 0, 1 << 20) % (room + 1)
    lengths = lengths.at[1:1 + 2 * twos:2].set(source_of - moved).at[2:2 + 2 * twos:2].set(sink + moved)
    return lengths[jax.random.permutation(jax.random.fold_in(own_key, 2), number_of)]


def bell_draw(key, dims, scale, bound, shards=(), kind=jnp.bfloat16):
    entries = scale * jax.random.normal(key, dims, jnp.float32)
    if shards:
        entries = entries * levels(key, dims, shards, -0.22, 0.18)
    return jnp.clip(entries, -bound, bound).astype(kind)


def gaussian_with(rng, extent, spread, reach, shards, heavy, kind=jnp.bfloat16):
    values = spread * jax.random.normal(rng, extent, jnp.float32)
    if shards:
        values = values * levels(rng, extent, shards, -0.22, 0.18)
    return jnp.clip(with_spikes(values, jax.random.fold_in(rng, 3), *heavy), -reach, reach).astype(kind)


def setup_inputs(seed: int = 0) -> dict:
    seeds = jax.random.split(jax.random.key(seed), 6)
    return {
        "rotated_queries": draw_rotated_queries(jax.random.fold_in(seeds[5], 71), 0),
        "rotated_keys": draw_rotated_keys(jax.random.fold_in(seeds[5], 71), 0),
        "projected_values": bell_draw(seeds[2], (PACK_TOKENS, KEY_VALUE_HEADS * HEAD_SIZE), 1.0, 6.0, ((0, 64), (1, 4))),
        "doc_ids": jnp.searchsorted(jnp.cumsum(uneven_parts(seeds[3], DOCS, PACK_TOKENS, MAXDOC, 2)), jnp.arange(PACK_TOKENS), side="right").astype(jnp.int32),
        "w_out": gaussian_with(seeds[4], (QUERY_HEADS * HEAD_SIZE, DOUT), (QUERY_HEADS * HEAD_SIZE) ** -0.5, 0.125, ((0, 4),), (0, 1, 4, 2.0)),
    }


masked_value = -1e+30

def reference(rotated_queries, rotated_keys, projected_values, doc_ids, w_out):
    query_group = QUERY_HEADS // KEY_VALUE_HEADS
    score_scale = 1.0 / math.sqrt(HEAD_SIZE)
    padding_length = MAXDOC
    span_length = MAXDOC + TOKENS_PER_SHARD
    padded_key_rows = jnp.concatenate([jnp.zeros((padding_length, KEY_VALUE_HEADS * HEAD_SIZE), jnp.bfloat16), rotated_keys], axis=0)
    padded_value_rows = jnp.concatenate([jnp.zeros((padding_length, KEY_VALUE_HEADS * HEAD_SIZE), jnp.bfloat16), projected_values], axis=0)
    doc_marks = (doc_ids + 1).astype(jnp.int32)
    marks_padded = jnp.concatenate([jnp.zeros((padding_length,), jnp.int32), doc_marks], axis=0)

    def query_block(which):
        token_offset = (which * TOKENS_PER_SHARD).astype(jnp.int32)
        query_rows = lax.dynamic_slice_in_dim(rotated_queries, token_offset, TOKENS_PER_SHARD, 0).reshape(TOKENS_PER_SHARD, KEY_VALUE_HEADS, query_group, HEAD_SIZE).astype(jnp.float32)
        key_rows = lax.dynamic_slice_in_dim(padded_key_rows, token_offset, span_length, 0).reshape(span_length, KEY_VALUE_HEADS, HEAD_SIZE).astype(jnp.float32)
        value_rows = lax.dynamic_slice_in_dim(padded_value_rows, token_offset, span_length, 0).reshape(span_length, KEY_VALUE_HEADS, HEAD_SIZE).astype(jnp.float32)
        query_marks = lax.dynamic_slice_in_dim(doc_marks, token_offset, TOKENS_PER_SHARD, 0)
        key_marks = lax.dynamic_slice_in_dim(marks_padded, token_offset, span_length, 0)
        key_pos = jnp.arange(span_length, dtype=jnp.int32) - padding_length
        query_pos = jnp.arange(TOKENS_PER_SHARD, dtype=jnp.int32)
        scores = jnp.einsum('tkgd,skd->kgts', query_rows, key_rows, precision=lax.Precision.HIGHEST) * score_scale
        visible = (key_marks[None, :] == query_marks[:, None]) & (key_pos[None, :] <= query_pos[:, None])
        top = lax.optimization_barrier(jnp.max(jnp.where(visible, scores, masked_value), axis=-1))
        weights = jnp.where(visible, jnp.exp(scores - top[..., None]), 0.0)
        total = lax.optimization_barrier(jnp.sum(weights, axis=-1))
        rounded = lax.optimization_barrier(weights.astype(jnp.bfloat16)).astype(jnp.float32)
        summed = jnp.einsum('kgts,skd->kgtd', rounded, value_rows, precision=lax.Precision.HIGHEST)
        result = summed / total[..., None]
        return result.transpose(2, 0, 1, 3).reshape(TOKENS_PER_SHARD, QUERY_HEADS * HEAD_SIZE).astype(jnp.bfloat16)
    attended = lax.map(query_block, jnp.arange(PACK_TOKENS // TOKENS_PER_SHARD, dtype=jnp.int32)).reshape(PACK_TOKENS, QUERY_HEADS * HEAD_SIZE)
    width = QUERY_HEADS * HEAD_SIZE // N_HEAD
    mixed = jnp.zeros((PACK_TOKENS, DOUT), jnp.float32)
    for index in range(N_HEAD):
        features = attended[:, index * width:(index + 1) * width]
        rows = w_out[index * width:(index + 1) * width, :]
        partial_value = jnp.dot(features, rows, preferred_element_type=jnp.float32).astype(jnp.bfloat16)
        mixed = mixed + partial_value.astype(jnp.float32)
    return mixed.astype(jnp.bfloat16)
```

```python
import functools
import math

import jax
import jax.numpy as jnp
from jax import lax
from jax.experimental import pallas as pl
from jax.experimental.pallas import tpu as pltpu
from jax.sharding import PartitionSpec as P

MESH = pl.DeviceIdType.MESH
HD = 128
ROWS = 256
HEADS = 8
BACK = 8
COLS = 640
HIDDEN = -1e30
RATE = math.log2(math.e) / math.sqrt(HD)
CHUNKS = 4
TOK = ROWS // CHUNKS
MSG = 272


def wide(x, n):
    return jnp.concatenate([x] * n, axis=1)


def kernel(n_ctx, q_hbm, k_ref, v_ref, ids_ref, w_hbm, o_ref,
           q, w, own, got, kaug, vaug, qaug, dmask, acc, top, att, keep,
           core_out, core_in, y_out, y_in,
           load_sem, w_sem, send_sem, recv_sem, cs_sem, cr_sem, ys_sem, yr_sem):
    ctx = lax.axis_index("ctx")
    head = lax.axis_index("head")
    y_hi, core = head // 2, lax.rem(head, 2)
    mate = y_hi * 2 + (1 - core)
    far = (1 - y_hi) * 2 + core

    barrier = pltpu.get_barrier_semaphore()
    for j in range(1, BACK + 1):
        @pl.when(ctx - j >= 0)
        def _():
            pl.semaphore_signal(barrier, inc=1, device_id=(ctx - j, head), device_id_type=MESH)
    pl.semaphore_signal(barrier, inc=1, device_id=(ctx, mate), device_id_type=MESH)
    pl.semaphore_signal(barrier, inc=1, device_id=(ctx, far), device_id_type=MESH)

    q_load = pltpu.make_async_copy(q_hbm, q, load_sem)
    q_load.start()
    w_loads = []
    groups = [(1 - y_hi) * 2 + (1 - core), y_hi * 2 + (1 - core), (1 - y_hi) * 2 + core, y_hi * 2 + core]
    for i, g in enumerate(groups):
        c = pltpu.make_async_copy(
            w_hbm.at[:, pl.ds(pl.multiple_of(g * COLS, 128), COLS)], w.at[:, pl.ds(i * COLS, COLS)], w_sem.at[i])
        c.start()
        w_loads.append(c)

    ids = ids_ref[...].astype(jnp.float32)
    own[0:HD, :] = k_ref[...].T
    own[HD:HD + 16, :] = jnp.broadcast_to(ids, (16, ROWS)).astype(jnp.bfloat16)
    own[HD + 16:, 0:HD] = v_ref[0:HD, :]
    own[HD + 16:, HD:] = v_ref[HD:, :]

    reach = jnp.minimum(n_ctx - 1 - ctx, BACK)
    pl.semaphore_wait(barrier, reach + 2)

    def kv_copy(j):
        return pltpu.make_async_remote_copy(
            src_ref=own, dst_ref=got.at[j - 1], send_sem=send_sem.at[j - 1], recv_sem=recv_sem.at[j - 1],
            device_id=(lax.rem(ctx + j, n_ctx), head), device_id_type=MESH)

    for j in range(1, BACK + 1):
        @pl.when(ctx + j < n_ctx)
        def _():
            kv_copy(j).start()

    ids_col = jnp.broadcast_to(ids, (HD, ROWS)).T
    first = ids[0:1, 0:1]
    lane = lax.broadcasted_iota(jnp.int32, (ROWS, HD), 1)
    other_doc = jnp.where(ids_col == first, 0.0, 1.0)
    qaug[...] = jnp.where(lane == 0, 1.0, jnp.where(lane == 1, other_doc, 0.0)).astype(jnp.bfloat16)
    t_pos = lax.broadcasted_iota(jnp.int32, (ROWS, ROWS), 0)
    s_pos = lax.broadcasted_iota(jnp.int32, (ROWS, ROWS), 1)
    seen = (wide(ids_col, 2) == ids) & (s_pos <= t_pos)
    dmask[...] = jnp.where(seen, 0.0, HIDDEN)
    kaug[HD + 16:, :] = jnp.zeros((HD - 16, 2 * ROWS), jnp.bfloat16)
    vaug[:, HD:] = jnp.ones((2 * ROWS, HD), jnp.bfloat16)

    vaug[0:HD, 0:HD] = v_ref[0:HD, :]
    vaug[HD:ROWS, 0:HD] = v_ref[HD:, :]
    q_load.wait()

    def cols(h):
        return pl.ds(pl.multiple_of(h * HD, HD), HD)

    @pl.loop(0, HEADS)
    def _(h):
        s = jnp.dot(q[:, cols(h)], own[0:HD, :], preferred_element_type=jnp.float32) + dmask[...]
        m = jnp.broadcast_to(jnp.max(s, axis=1, keepdims=True), (ROWS, HD))
        p = jnp.exp2((s - wide(m, 2)) * RATE).astype(jnp.bfloat16)
        acc[h] = jnp.dot(p, vaug[0:ROWS, :], preferred_element_type=jnp.float32)
        top[h] = m

    def fill(j, place):
        rows = pl.ds(place * ROWS, ROWS)
        msg = got.at[j - 1]
        kaug[0:HD, rows] = msg[0:HD, :]
        bias = jnp.where(msg[HD:HD + 16, :].astype(jnp.float32) == first, 0.0, HIDDEN)
        row = lax.broadcasted_iota(jnp.int32, (16, ROWS), 0)
        kaug[HD:HD + 16, rows] = jnp.where(row == 0, bias, jnp.where(row == 1, HIDDEN, 0.0)).astype(jnp.bfloat16)
        vaug[place * ROWS:place * ROWS + HD, 0:HD] = msg[HD + 16:, 0:HD]
        vaug[place * ROWS + HD:(place + 1) * ROWS, 0:HD] = msg[HD + 16:, HD:]

    def arrive(j):
        @pl.when(ctx >= j)
        def _():
            kv_copy(j).wait_recv()

        @pl.when(ctx < j)
        def _():
            got[j - 1] = jnp.full((MSG, ROWS), -1.0, jnp.bfloat16)

    def step(h, toks, n):
        left = jnp.concatenate([q[toks, cols(h)], qaug[toks, :]], axis=1)
        s = jnp.dot(left, kaug[...], preferred_element_type=jnp.float32)
        old = top[h, toks, :]
        m = jnp.maximum(old, jnp.broadcast_to(jnp.max(s, axis=1, keepdims=True), (n, HD)))
        p = jnp.exp2((s - wide(m, 4)) * RATE).astype(jnp.bfloat16)
        shrink = jnp.exp2((old - m) * RATE)
        total = acc[h, toks, :] * wide(shrink, 2) + jnp.dot(p, vaug[...], preferred_element_type=jnp.float32)
        return m, total

    for pair in range(BACK // 2):
        for place in range(2):
            j = 2 * pair + place + 1
            arrive(j)
            fill(j, place)
        if pair < BACK // 2 - 1:
            @pl.loop(0, HEADS)
            def _(h):
                m, total = step(h, pl.ds(0, ROWS), ROWS)
                top[h] = m
                acc[h] = total

    for c in w_loads:
        c.wait()

    def core_copy(i):
        return pltpu.make_async_remote_copy(
            src_ref=core_out.at[i], dst_ref=core_in.at[i], send_sem=cs_sem.at[i], recv_sem=cr_sem.at[i],
            device_id=(ctx, mate), device_id_type=MESH)

    def y_copy(i):
        return pltpu.make_async_remote_copy(
            src_ref=y_out.at[i], dst_ref=y_in.at[i], send_sem=ys_sem.at[i], recv_sem=yr_sem.at[i],
            device_id=(ctx, far), device_id_type=MESH)

    def relay(i):
        core_copy(i).wait_recv()
        y_out[i] = (keep[i, :, 0:COLS] + core_in[i, :, 0:COLS].astype(jnp.float32)).astype(jnp.bfloat16)
        y_copy(i).start()

    for i in range(CHUNKS):
        toks = pl.ds(i * TOK, TOK)

        @pl.loop(0, HEADS)
        def _(h):
            _, total = step(h, toks, TOK)
            att[:, cols(h)] = (total[:, 0:HD] / total[:, HD:]).astype(jnp.bfloat16)

        core_out[i] = jnp.dot(att[...], w[:, 0:2 * COLS], preferred_element_type=jnp.float32).astype(jnp.bfloat16)
        core_copy(i).start()
        keep[i] = jnp.dot(att[...], w[:, 2 * COLS:], preferred_element_type=jnp.float32)
        if i > 0:
            relay(i - 1)
    relay(CHUNKS - 1)

    for i in range(CHUNKS):
        y_copy(i).wait_recv()
        mine = keep[i, :, COLS:] + core_in[i, :, COLS:].astype(jnp.float32)
        o_ref[i * TOK:(i + 1) * TOK, :] = (mine + y_in[i].astype(jnp.float32)).astype(jnp.bfloat16)

    for i in range(CHUNKS):
        core_copy(i).wait_send()
        y_copy(i).wait_send()
    for j in range(1, BACK + 1):
        @pl.when(ctx + j < n_ctx)
        def _():
            kv_copy(j).wait_send()


def solution(mesh):
    n_ctx = mesh.shape["ctx"]

    def local(queries, keys, values, doc_ids, w_out):
        vmem = pl.BlockSpec(memory_space=pltpu.VMEM)
        hbm = pl.BlockSpec(memory_space=pl.ANY)
        bf16, f32 = jnp.bfloat16, jnp.float32
        return pl.pallas_call(
            functools.partial(kernel, n_ctx),
            out_shape=jax.ShapeDtypeStruct((ROWS, COLS), bf16),
            in_specs=[hbm, vmem, vmem, vmem, hbm],
            out_specs=vmem,
            scratch_shapes=[
                pltpu.VMEM((ROWS, HEADS * HD), bf16),
                pltpu.VMEM((HEADS * HD, 4 * COLS), bf16),
                pltpu.VMEM((MSG, ROWS), bf16),
                pltpu.VMEM((BACK, MSG, ROWS), bf16),
                pltpu.VMEM((2 * HD, 2 * ROWS), bf16),
                pltpu.VMEM((2 * ROWS, 2 * HD), bf16),
                pltpu.VMEM((ROWS, HD), bf16),
                pltpu.VMEM((ROWS, ROWS), f32),
                pltpu.VMEM((HEADS, ROWS, 2 * HD), f32),
                pltpu.VMEM((HEADS, ROWS, HD), f32),
                pltpu.VMEM((TOK, HEADS * HD), bf16),
                pltpu.VMEM((CHUNKS, TOK, 2 * COLS), f32),
                pltpu.VMEM((CHUNKS, TOK, 2 * COLS), bf16),
                pltpu.VMEM((CHUNKS, TOK, 2 * COLS), bf16),
                pltpu.VMEM((CHUNKS, TOK, COLS), bf16),
                pltpu.VMEM((CHUNKS, TOK, COLS), bf16),
                pltpu.SemaphoreType.DMA,
                pltpu.SemaphoreType.DMA((4,)),
                pltpu.SemaphoreType.DMA((BACK,)),
                pltpu.SemaphoreType.DMA((BACK,)),
                pltpu.SemaphoreType.DMA((CHUNKS,)),
                pltpu.SemaphoreType.DMA((CHUNKS,)),
                pltpu.SemaphoreType.DMA((CHUNKS,)),
                pltpu.SemaphoreType.DMA((CHUNKS,)),
            ],
            compiler_params=pltpu.CompilerParams(
                collective_id=0, has_side_effects=True, vmem_limit_bytes=48 * 2**20),
        )(queries, keys, values, doc_ids.reshape(1, ROWS), w_out)

    placed = (P("ctx", "head"), P("ctx", "head"), P("ctx", "head"), P("ctx"), P("head", None))
    return jax.shard_map(local, mesh=mesh, in_specs=placed, out_specs=P("ctx", "head"), check_vma=False)
```

```python
import functools
import math

import jax
import jax.numpy as jnp
from jax import lax
from jax.experimental import pallas as pl
from jax.experimental.pallas import tpu as pltpu
from jax.sharding import PartitionSpec as P

MESH = pl.DeviceIdType.MESH
HD = 128
ROWS = 256
HEADS = 8
COLS = 640
HIDDEN = -1e30
RATE = math.log2(math.e) / math.sqrt(HD)
CHUNKS = 2
TOK = ROWS // CHUNKS
KEY_ROWS = HD + 16
MSG = KEY_ROWS + HD
SLOTS = 8
BEHIND, ROW, LEFT, RIGHT, ROW_LEFT, ROW_RIGHT, ACROSS, ROW_ACROSS = range(SLOTS)
RING = 4
FAR, NEAR = range(2)
PART = 256
PARTS = HEADS * TOK // PART


def wide(x, n):
    return jnp.concatenate([x] * n, axis=1)


def kernel(n_ctx, q_hbm, k_hbm, v_hbm, ids_hbm, w_hbm, o_ref,
           q, k, v, marks, w, own, got, rows, kaug, vaug, acc, top, att, keep,
           core_out, core_in, y_out, y_in,
           load_sem, w_sem, send_sem, recv_sem, cs_sem, cr_sem, ys_sem, yr_sem):
    ctx = lax.axis_index("ctx")
    head = lax.axis_index("head")
    y_hi, core = head // 2, lax.rem(head, 2)
    x = lax.rem(ctx, RING)
    base = ctx - x
    y_lo = lax.rem(ctx // RING, 2)
    upper, lower = y_lo == 0, y_lo == 1
    inner = (x == 1) | (x == 2)
    outer = jnp.logical_not(inner)
    x_right, x_left, x_over = lax.rem(x + 1, RING), lax.rem(x + RING - 1, RING), lax.rem(x + 2, RING)
    right, left, over = base + x_right, base + x_left, base + x_over
    have_behind, have_row = ctx >= 2 * RING, ctx >= RING
    give_behind, give_row = ctx + 2 * RING < n_ctx, ctx + RING < n_ctx
    mate = y_hi * 2 + (1 - core)
    far = (1 - y_hi) * 2 + core

    barrier = pltpu.get_barrier_semaphore()

    def greet(where, c, h):
        @pl.when(where)
        def _():
            pl.semaphore_signal(barrier, inc=1, device_id=(c, h), device_id_type=MESH)

    greet(have_behind, ctx - 2 * RING, head)
    for c in (x, x_left, x_right):
        greet(have_row, base - RING + c, head)
    for c, h in ((left, head), (right, head), (over, head), (ctx, mate), (ctx, far)):
        greet(True, c, h)

    loads = [pltpu.make_async_copy(src, dst, load_sem.at[i])
             for i, (src, dst) in enumerate([(k_hbm, k), (v_hbm, v), (ids_hbm, marks), (q_hbm, q)])]
    for c in loads:
        c.start()
    for c in loads[:3]:
        c.wait()

    ids = marks[...].astype(jnp.float32)
    own[0:HD, :] = k[...].T
    own[HD:HD + 16, :] = jnp.broadcast_to(ids, (16, ROWS)).astype(jnp.bfloat16)
    own[KEY_ROWS:, 0:HD] = v[0:HD, :]
    own[KEY_ROWS:, HD:] = v[HD:, :]

    greeted = 5 + give_behind.astype(jnp.int32) + 3 * give_row.astype(jnp.int32)
    pl.semaphore_wait(barrier, greeted)

    sent = []

    def send(where, src, slot, lane, dest):
        copy = pltpu.make_async_remote_copy(
            src_ref=own if src is None else got.at[src], dst_ref=got.at[slot],
            send_sem=send_sem.at[lane], recv_sem=recv_sem.at[slot],
            device_id=(dest, head), device_id_type=MESH)

        @pl.when(where)
        def _():
            copy.start()

        sent.append((where, copy))

    def arrive(slot, where):
        @pl.when(where)
        def _():
            pltpu.make_async_remote_copy(
                src_ref=own, dst_ref=got.at[slot], send_sem=send_sem.at[0],
                recv_sem=recv_sem.at[slot], device_id=(left, head), device_id_type=MESH).wait_recv()

        @pl.when(jnp.logical_not(where))
        def _():
            got[slot] = jnp.full((MSG, ROWS), -1.0, jnp.bfloat16)

    ahead, next_base = lax.rem(ctx + 2 * RING, n_ctx), lax.rem(base + RING, n_ctx)
    send(give_behind, None, BEHIND, 0, ahead)
    send(give_row, None, ROW, 1, next_base + x)
    send(x < RING - 1, None, LEFT, 2, right)
    send(x == 0, None, RIGHT, 3, left)

    w_loads = []
    groups = [(1 - y_hi) * 2 + (1 - core), (1 - y_hi) * 2 + core, y_hi * 2 + (1 - core), y_hi * 2 + core]
    for i, g in enumerate(groups):
        c = pltpu.make_async_copy(
            w_hbm.at[:, pl.ds(pl.multiple_of(g * COLS, 128), COLS)], w.at[:, pl.ds(i * COLS, COLS)], w_sem.at[i])
        c.start()
        w_loads.append(c)

    ids_col = jnp.broadcast_to(ids, (HD, ROWS)).T
    first = ids[0:1, 0:1]
    lane = lax.broadcasted_iota(jnp.int32, (ROWS, HD), 1)
    other_doc = jnp.where(ids_col == first, 0.0, 1.0)
    qaug = jnp.where(lane == 0, 1.0, jnp.where(lane == 1, other_doc, 0.0)).astype(jnp.bfloat16)
    t_pos = lax.broadcasted_iota(jnp.int32, (ROWS, ROWS), 0)
    s_pos = lax.broadcasted_iota(jnp.int32, (ROWS, ROWS), 1)
    seen = (wide(ids_col, 2) == ids) & (s_pos <= t_pos)
    dmask = jnp.where(seen, 0.0, HIDDEN)
    kaug[:, HD + 16:, :] = jnp.zeros((2, HD - 16, 2 * ROWS), jnp.bfloat16)
    vaug[:, :, HD:] = jnp.ones((2, 2 * ROWS, HD), jnp.bfloat16)
    vaug[1, 0:HD, 0:HD] = v[0:HD, :]
    vaug[1, HD:ROWS, 0:HD] = v[HD:, :]

    loads[3].wait()
    for c in range(CHUNKS):
        for h in range(HEADS):
            at = (c * HEADS + h) * TOK
            rows[at:at + TOK, 0:HD] = q[c * TOK:(c + 1) * TOK, h * HD:(h + 1) * HD]
            rows[at:at + TOK, HD:] = qaug[c * TOK:(c + 1) * TOK, :]

    for c in range(CHUNKS):
        seen_keys = (c + 1) * TOK
        mask = jnp.concatenate([dmask[c * TOK:(c + 1) * TOK, 0:seen_keys]] * (PART // TOK), axis=0)
        for i in range(c * PARTS, (c + 1) * PARTS):
            here = pl.ds(i * PART, PART)
            s = jnp.dot(rows[here, 0:HD], own[0:HD, 0:seen_keys], preferred_element_type=jnp.float32) + mask
            m = jnp.broadcast_to(jnp.max(s, axis=1, keepdims=True), (PART, HD))
            p = jnp.exp2((s - wide(m, seen_keys // HD)) * RATE).astype(jnp.bfloat16)
            acc[here, :] = jnp.dot(p, vaug[1, 0:seen_keys, :], preferred_element_type=jnp.float32)
            top[here, :] = m

    def fill(slot, b, place):
        cols = pl.ds(place * ROWS, ROWS)
        msg = got.at[slot]
        kaug[b, 0:HD, cols] = msg[0:HD, :]
        bias = jnp.where(msg[HD:HD + 16, :].astype(jnp.float32) == first, 0.0, HIDDEN)
        row = lax.broadcasted_iota(jnp.int32, (16, ROWS), 0)
        kaug[b, HD:HD + 16, cols] = jnp.where(row == 0, bias, jnp.where(row == 1, HIDDEN, 0.0)).astype(jnp.bfloat16)
        vaug[b, place * ROWS:place * ROWS + HD, 0:HD] = msg[KEY_ROWS:, 0:HD]
        vaug[b, place * ROWS + HD:(place + 1) * ROWS, 0:HD] = msg[KEY_ROWS:, HD:]

    def step(here, b):
        s = jnp.dot(rows[here, :], kaug[b], preferred_element_type=jnp.float32)
        old = top[here, :]
        m = jnp.maximum(old, jnp.broadcast_to(jnp.max(s, axis=1, keepdims=True), (PART, HD)))
        p = jnp.exp2((s - wide(m, 4)) * RATE).astype(jnp.bfloat16)
        shrink = jnp.exp2((old - m) * RATE)
        total = acc[here, :] * wide(shrink, 2) + jnp.dot(p, vaug[b], preferred_element_type=jnp.float32)
        return m, total

    def fold(b):
        for i in range(CHUNKS * PARTS):
            here = pl.ds(i * PART, PART)
            m, total = step(here, b)
            top[here, :] = m
            acc[here, :] = total

    arrive(BEHIND, have_behind)
    send(have_behind & (x > 0), BEHIND, RIGHT, 4, left)
    send(have_behind & (x == RING - 1), BEHIND, LEFT, 5, right)
    arrive(ROW, have_row)
    send(have_row, ROW, ROW_LEFT, 6, right)
    send(have_row, ROW, ROW_RIGHT, 7, left)
    arrive(LEFT, have_behind | (x > 0))
    send(inner, LEFT, ACROSS, 8, right)
    fill(BEHIND, 0, 0)
    fill(ROW, 0, 1)
    fold(0)
    arrive(RIGHT, have_behind | (x == RING - 1))
    send(inner & have_behind, RIGHT, ACROSS, 9, left)
    arrive(ROW_LEFT, have_row)
    send(outer & have_row, ROW_LEFT, ROW_ACROSS, 10, right)
    arrive(ROW_RIGHT, have_row)
    send(outer & have_row, ROW_RIGHT, ROW_ACROSS, 11, left)
    fill(LEFT, 1, 0)
    fill(ROW_LEFT, 1, 1)
    fold(1)
    fill(RIGHT, 0, 0)
    fill(ROW_RIGHT, 0, 1)
    fold(0)
    arrive(ACROSS, have_behind | (x > 1))
    arrive(ROW_ACROSS, have_row)
    fill(ACROSS, 1, 0)
    fill(ROW_ACROSS, 1, 1)

    for c in w_loads:
        c.wait()

    def core_copy(side, c):
        return pltpu.make_async_remote_copy(
            src_ref=core_out.at[side, c], dst_ref=core_in.at[side, c], send_sem=cs_sem.at[side, c],
            recv_sem=cr_sem.at[side, c], device_id=(ctx, mate), device_id_type=MESH)

    def y_copy(c):
        return pltpu.make_async_remote_copy(
            src_ref=y_out.at[c], dst_ref=y_in.at[c], send_sem=ys_sem.at[c], recv_sem=yr_sem.at[c],
            device_id=(ctx, far), device_id_type=MESH)

    def finish(c):
        for i in range(PARTS):
            _, total = step(pl.ds((c * PARTS + i) * PART, PART), 1)
            mean = (total[:, 0:HD] / total[:, HD:]).astype(jnp.bfloat16)
            for n in range(PART // TOK):
                h = i * (PART // TOK) + n
                att[c, :, h * HD:(h + 1) * HD] = mean[n * TOK:(n + 1) * TOK, :]

    def project(side, c):
        at = 2 * side * COLS
        core_out[side, c] = jnp.dot(
            att[c], w[:, at:at + COLS], preferred_element_type=jnp.float32).astype(jnp.bfloat16)
        core_copy(side, c).start()
        keep[side, c] = jnp.dot(att[c], w[:, at + COLS:at + 2 * COLS], preferred_element_type=jnp.float32)

    def relay(c):
        core_copy(FAR, c).wait_recv()
        y_out[c] = (keep[FAR, c] + core_in[FAR, c].astype(jnp.float32)).astype(jnp.bfloat16)
        y_copy(c).start()

    finish(0)
    project(FAR, 0)
    finish(1)
    relay(0)
    project(FAR, 1)
    project(NEAR, 0)
    relay(1)
    project(NEAR, 1)

    for c in range(CHUNKS):
        core_copy(NEAR, c).wait_recv()
        keep[NEAR, c] += core_in[NEAR, c].astype(jnp.float32)
    for c in range(CHUNKS):
        y_copy(c).wait_recv()
        o_ref[c * TOK:(c + 1) * TOK, :] = (keep[NEAR, c] + y_in[c].astype(jnp.float32)).astype(jnp.bfloat16)

    for c in range(CHUNKS):
        core_copy(FAR, c).wait_send()
        core_copy(NEAR, c).wait_send()
        y_copy(c).wait_send()
    for where, copy in sent:
        @pl.when(where)
        def _():
            copy.wait_send()


def solution(mesh):
    n_ctx = mesh.shape["ctx"]

    def local(queries, keys, values, doc_ids, w_out):
        hbm = pl.BlockSpec(memory_space=pltpu.HBM)
        bf16, f32 = jnp.bfloat16, jnp.float32
        vmem, dma = pltpu.VMEM, pltpu.SemaphoreType.DMA
        return pl.pallas_call(
            functools.partial(kernel, n_ctx),
            out_shape=pltpu.VMEM((ROWS, COLS), bf16),
            in_specs=[hbm] * 5,
            out_specs=pl.BlockSpec(memory_space=pltpu.VMEM),
            scratch_shapes=[
                vmem((ROWS, HEADS * HD), bf16),
                vmem((ROWS, HD), bf16),
                vmem((ROWS, HD), bf16),
                vmem((1, ROWS), jnp.int32),
                vmem((HEADS * HD, 4 * COLS), bf16),
                vmem((MSG, ROWS), bf16),
                vmem((SLOTS, MSG, ROWS), bf16),
                vmem((HEADS * ROWS, 2 * HD), bf16),
                vmem((2, 2 * HD, 2 * ROWS), bf16),
                vmem((2, 2 * ROWS, 2 * HD), bf16),
                vmem((HEADS * ROWS, 2 * HD), f32),
                vmem((HEADS * ROWS, HD), f32),
                vmem((CHUNKS, TOK, HEADS * HD), bf16),
                vmem((2, CHUNKS, TOK, COLS), f32),
                vmem((2, CHUNKS, TOK, COLS), bf16),
                vmem((2, CHUNKS, TOK, COLS), bf16),
                vmem((CHUNKS, TOK, COLS), bf16),
                vmem((CHUNKS, TOK, COLS), bf16),
                dma((4,)),
                dma((4,)),
                dma((12,)),
                dma((SLOTS,)),
                dma((2, CHUNKS)),
                dma((2, CHUNKS)),
                dma((CHUNKS,)),
                dma((CHUNKS,)),
            ],
            compiler_params=pltpu.CompilerParams(
                collective_id=0, has_side_effects=True, vmem_limit_bytes=63 * 2**20),
        )(queries, keys, values, doc_ids.reshape(1, ROWS), w_out)

    placed = (P("ctx", "head"), P("ctx", "head"), P("ctx", "head"), P("ctx"), P("head", None))
    return jax.shard_map(local, mesh=mesh, in_specs=placed, out_specs=P("ctx", "head"), check_vma=False)
```

```python
import functools
import math

import jax
import jax.numpy as jnp
from jax import lax
from jax.experimental import pallas as pl
from jax.experimental.pallas import tpu as pltpu
from jax.sharding import PartitionSpec as P

MESH = pl.DeviceIdType.MESH
HD = 128
ROWS = 256
HEADS = 8
COLS = 640
HIDDEN = -1e30
RATE = math.log2(math.e) / math.sqrt(HD)
CHUNKS = ((0, 64), (64, 64), (128, 128))
KEY_ROWS = HD + 16
MSG = KEY_ROWS + HD
SLOTS = 8
BEHIND, ROW, LEFT, RIGHT, ROW_LEFT, ROW_RIGHT, ACROSS, ROW_ACROSS = range(SLOTS)
PASS_LEFT, PASS_RIGHT = SLOTS, SLOTS + 1
RING = 4
FAR, NEAR = range(2)
PART = 256


def wide(x, n):
    return jnp.concatenate([x] * n, axis=1)


def kernel(n_ctx, q_hbm, k_hbm, v_hbm, ids_hbm, w_hbm, o_ref,
           q, k, v, marks, w, own, got, rows, kaug, vaug, acc, top, att, keep,
           core_out, core_in, y_out, y_in,
           load_sem, w_sem, send_sem, recv_sem, cs_sem, cr_sem, ys_sem, yr_sem):
    ctx = lax.axis_index("ctx")
    head = lax.axis_index("head")
    y_hi, core = head // 2, lax.rem(head, 2)
    x = lax.rem(ctx, RING)
    base = ctx - x
    inner = (x == 1) | (x == 2)
    outer = jnp.logical_not(inner)
    right, left = base + lax.rem(x + 1, RING), base + lax.rem(x + RING - 1, RING)
    have_behind, have_row = ctx >= 2 * RING, ctx >= RING
    give_behind, give_row = ctx + 2 * RING < n_ctx, ctx + RING < n_ctx
    mate = y_hi * 2 + (1 - core)
    far = (1 - y_hi) * 2 + core

    barrier = pltpu.get_barrier_semaphore()

    def greet(where, c, h):
        @pl.when(where)
        def _():
            pl.semaphore_signal(barrier, inc=1, device_id=(c, h), device_id_type=MESH)

    greet(have_behind, ctx - 2 * RING, head)
    greet(have_row, ctx - RING, head)
    for c, h in ((left, head), (right, head), (ctx, mate), (ctx, far)):
        greet(True, c, h)

    loads = [pltpu.make_async_copy(src, dst, load_sem.at[i])
             for i, (src, dst) in enumerate([(k_hbm, k), (v_hbm, v), (ids_hbm, marks), (q_hbm, q)])]
    for c in loads:
        c.start()
    for c in loads[:3]:
        c.wait()

    ids = marks[...].astype(jnp.float32)
    own[0:HD, :] = k[...].T
    own[HD:HD + 16, :] = jnp.broadcast_to(ids, (16, ROWS)).astype(jnp.bfloat16)
    own[KEY_ROWS:, 0:HD] = v[0:HD, :]
    own[KEY_ROWS:, HD:] = v[HD:, :]

    greeted = 4 + give_behind.astype(jnp.int32) + give_row.astype(jnp.int32)
    pl.semaphore_wait(barrier, greeted)

    sent = []

    def send(where, src, slot, lane, dest):
        copy = pltpu.make_async_remote_copy(
            src_ref=own if src is None else got.at[src], dst_ref=got.at[slot],
            send_sem=send_sem.at[lane], recv_sem=recv_sem.at[slot],
            device_id=(dest, head), device_id_type=MESH)

        @pl.when(where)
        def _():
            copy.start()

        sent.append((where, copy))

    def arrive(slot, where):
        @pl.when(where)
        def _():
            pltpu.make_async_remote_copy(
                src_ref=own, dst_ref=got.at[slot], send_sem=send_sem.at[0],
                recv_sem=recv_sem.at[slot], device_id=(left, head), device_id_type=MESH).wait_recv()

    def blank(slot, where):
        @pl.when(where)
        def _():
            got[slot] = jnp.full((MSG, ROWS), -1.0, jnp.bfloat16)

    for slot in (BEHIND, RIGHT, LEFT, ACROSS):
        here = {RIGHT: x < RING - 1, LEFT: x == 0, ACROSS: x < 2}.get(slot, True)
        blank(slot, jnp.logical_not(have_behind) & here)
    for slot in (ROW, ROW_LEFT, ROW_RIGHT, ROW_ACROSS):
        blank(slot, jnp.logical_not(have_row))

    ahead, below = lax.rem(ctx + 2 * RING, n_ctx), lax.rem(ctx + RING, n_ctx)
    send(give_row, None, ROW, 0, below)
    send((x > 0) & give_behind, None, PASS_RIGHT, 1, left)
    send(x < RING - 1, None, LEFT, 2, right)
    send((x == RING - 1) & give_behind, None, PASS_LEFT, 3, right)
    send(x == 0, None, RIGHT, 4, left)

    w_loads = []
    groups = [(1 - y_hi) * 2 + (1 - core), (1 - y_hi) * 2 + core, y_hi * 2 + (1 - core), y_hi * 2 + core]
    for i, g in enumerate(groups):
        c = pltpu.make_async_copy(
            w_hbm.at[:, pl.ds(pl.multiple_of(g * COLS, 128), COLS)], w.at[:, pl.ds(i * COLS, COLS)], w_sem.at[i])
        c.start()
        w_loads.append(c)

    ids_col = jnp.broadcast_to(ids, (HD, ROWS)).T
    first = ids[0:1, 0:1]
    lane = lax.broadcasted_iota(jnp.int32, (ROWS, HD), 1)
    other_doc = jnp.where(ids_col == first, 0.0, 1.0)
    qaug = jnp.where(lane == 0, 1.0, jnp.where(lane == 1, other_doc, 0.0)).astype(jnp.bfloat16)
    t_pos = lax.broadcasted_iota(jnp.int32, (ROWS, ROWS), 0)
    s_pos = lax.broadcasted_iota(jnp.int32, (ROWS, ROWS), 1)
    seen = (wide(ids_col, 2) == ids) & (s_pos <= t_pos)
    dmask = jnp.where(seen, 0.0, HIDDEN)
    kaug[:, HD + 16:, :] = jnp.zeros((2, HD - 16, 2 * ROWS), jnp.bfloat16)
    vaug[:, :, HD:] = jnp.ones((2, 2 * ROWS, HD), jnp.bfloat16)
    vaug[1, 0:HD, 0:HD] = v[0:HD, :]
    vaug[1, HD:ROWS, 0:HD] = v[HD:, :]

    loads[3].wait()
    for t, n in CHUNKS:
        for h in range(HEADS):
            at = t * HEADS + h * n
            rows[at:at + n, 0:HD] = q[t:t + n, h * HD:(h + 1) * HD]
            rows[at:at + n, HD:] = qaug[t:t + n, :]

    for t, n in CHUNKS:
        seen_keys = -(-(t + n) // HD) * HD
        mask = jnp.concatenate([dmask[t:t + n, 0:seen_keys]] * (PART // n), axis=0)
        for at in range(t * HEADS, (t + n) * HEADS, PART):
            here = pl.ds(at, PART)
            s = jnp.dot(rows[here, 0:HD], own[0:HD, 0:seen_keys], preferred_element_type=jnp.float32) + mask
            m = jnp.broadcast_to(jnp.max(s, axis=1, keepdims=True), (PART, HD))
            p = jnp.exp2((s - wide(m, seen_keys // HD)) * RATE).astype(jnp.bfloat16)
            acc[here, :] = jnp.dot(p, vaug[1, 0:seen_keys, :], preferred_element_type=jnp.float32)
            top[here, :] = m

    def fill(slot, b, place):
        cols = pl.ds(place * ROWS, ROWS)
        msg = got.at[slot]
        kaug[b, 0:HD, cols] = msg[0:HD, :]
        bias = jnp.where(msg[HD:HD + 16, :].astype(jnp.float32) == first, 0.0, HIDDEN)
        row = lax.broadcasted_iota(jnp.int32, (16, ROWS), 0)
        kaug[b, HD:HD + 16, cols] = jnp.where(row == 0, bias, jnp.where(row == 1, HIDDEN, 0.0)).astype(jnp.bfloat16)
        vaug[b, place * ROWS:place * ROWS + HD, 0:HD] = msg[KEY_ROWS:, 0:HD]
        vaug[b, place * ROWS + HD:(place + 1) * ROWS, 0:HD] = msg[KEY_ROWS:, HD:]

    def step(here, b, keys):
        s = jnp.dot(rows[here, :], kaug[b, :, 0:keys], preferred_element_type=jnp.float32)
        old = top[here, :]
        m = jnp.maximum(old, jnp.broadcast_to(jnp.max(s, axis=1, keepdims=True), (PART, HD)))
        p = jnp.exp2((s - wide(m, keys // HD)) * RATE).astype(jnp.bfloat16)
        shrink = jnp.exp2((old - m) * RATE)
        total = acc[here, :] * wide(shrink, 2) + jnp.dot(p, vaug[b, 0:keys, :], preferred_element_type=jnp.float32)
        return m, total

    def fold(b, keys=2 * ROWS):
        for at in range(0, HEADS * ROWS, PART):
            here = pl.ds(at, PART)
            m, total = step(here, b, keys)
            top[here, :] = m
            acc[here, :] = total

    send(give_behind, None, BEHIND, 5, ahead)
    arrive(ROW, have_row)
    send(have_row, ROW, ROW_LEFT, 8, right)
    send(have_row, ROW, ROW_RIGHT, 9, left)
    arrive(PASS_RIGHT, (x < RING - 1) & give_behind)
    send((x < RING - 1) & give_behind, PASS_RIGHT, RIGHT, 6, ahead)
    arrive(PASS_LEFT, (x == 0) & give_behind)
    send((x == 0) & give_behind, PASS_LEFT, LEFT, 7, ahead)
    arrive(LEFT, x > 0)
    send(inner, LEFT, ACROSS, 10, right)
    arrive(BEHIND, have_behind)
    fill(BEHIND, 0, 0)
    fill(ROW, 0, 1)
    fold(0)
    arrive(ROW_LEFT, outer & have_row)
    send(outer & have_row, ROW_LEFT, ROW_ACROSS, 12, right)
    arrive(ROW_RIGHT, outer & have_row)
    send(outer & have_row, ROW_RIGHT, ROW_ACROSS, 13, left)
    arrive(RIGHT, inner & have_behind)
    send(inner & have_behind, RIGHT, ACROSS, 11, left)
    arrive(LEFT, (x == 0) & have_behind)
    arrive(RIGHT, (x == RING - 1) | ((x == 0) & have_behind))
    fill(LEFT, 1, 0)
    fill(RIGHT, 1, 1)
    fold(1)
    arrive(ROW_LEFT, inner & have_row)
    arrive(ROW_RIGHT, inner & have_row)
    fill(ROW_LEFT, 0, 0)
    fill(ROW_RIGHT, 0, 1)
    fold(0)
    arrive(ACROSS, have_behind | (x > 1))
    fill(ACROSS, 1, 0)
    fold(1, ROWS)
    arrive(ROW_ACROSS, have_row)
    fill(ROW_ACROSS, 0, 0)

    for c in w_loads:
        c.wait()

    def core_copy(side, c):
        t, n = CHUNKS[c] if side == FAR else (0, ROWS)
        part = pl.ds(t, n)
        return pltpu.make_async_remote_copy(
            src_ref=core_out.at[side, part], dst_ref=core_in.at[side, part], send_sem=cs_sem.at[side, c],
            recv_sem=cr_sem.at[side, c], device_id=(ctx, mate), device_id_type=MESH)

    def y_copy(c):
        t, n = CHUNKS[c]
        part = pl.ds(t, n)
        return pltpu.make_async_remote_copy(
            src_ref=y_out.at[part], dst_ref=y_in.at[part], send_sem=ys_sem.at[c], recv_sem=yr_sem.at[c],
            device_id=(ctx, far), device_id_type=MESH)

    def finish(c):
        t, n = CHUNKS[c]
        for at in range(t * HEADS, (t + n) * HEADS, PART):
            _, total = step(pl.ds(at, PART), 0, ROWS)
            mean = (total[:, 0:HD] / total[:, HD:]).astype(jnp.bfloat16)
            for i in range(PART // n):
                h = (at - t * HEADS) // n + i
                att[t:t + n, h * HD:(h + 1) * HD] = mean[i * n:(i + 1) * n, :]

    def give(side, c):
        t, n = CHUNKS[c] if side == FAR else (0, ROWS)
        at = 2 * side * COLS
        core_out[side, t:t + n, :] = jnp.dot(
            att[t:t + n, :], w[:, at:at + COLS], preferred_element_type=jnp.float32).astype(jnp.bfloat16)
        core_copy(side, c).start()

    def hold(side, c):
        t, n = CHUNKS[c] if side == FAR else (0, ROWS)
        at = (2 * side + 1) * COLS
        keep[side, t:t + n, :] = jnp.dot(att[t:t + n, :], w[:, at:at + COLS], preferred_element_type=jnp.float32)

    def relay(c):
        t, n = CHUNKS[c]
        core_copy(FAR, c).wait_recv()
        y_out[t:t + n, :] = (keep[FAR, t:t + n, :] + core_in[FAR, t:t + n, :].astype(jnp.float32)).astype(jnp.bfloat16)
        y_copy(c).start()

    finish(0)
    give(FAR, 0)
    hold(FAR, 0)
    finish(1)
    give(FAR, 1)
    hold(FAR, 1)
    relay(0)
    finish(2)
    relay(1)
    give(FAR, 2)
    hold(FAR, 2)
    give(NEAR, 0)
    hold(NEAR, 0)
    relay(2)
    core_copy(NEAR, 0).wait_recv()
    keep[NEAR] += core_in[NEAR].astype(jnp.float32)
    for c, (t, n) in enumerate(CHUNKS):
        y_copy(c).wait_recv()
        o_ref[t:t + n, :] = (keep[NEAR, t:t + n, :] + y_in[t:t + n, :].astype(jnp.float32)).astype(jnp.bfloat16)

    core_copy(NEAR, 0).wait_send()
    for c in range(len(CHUNKS)):
        core_copy(FAR, c).wait_send()
        y_copy(c).wait_send()
    for where, copy in sent:
        @pl.when(where)
        def _():
            copy.wait_send()


def solution(mesh):
    n_ctx = mesh.shape["ctx"]

    def local(queries, keys, values, doc_ids, w_out):
        hbm = pl.BlockSpec(memory_space=pltpu.HBM)
        bf16, f32 = jnp.bfloat16, jnp.float32
        vmem, dma = pltpu.VMEM, pltpu.SemaphoreType.DMA
        return pl.pallas_call(
            functools.partial(kernel, n_ctx),
            out_shape=pltpu.VMEM((ROWS, COLS), bf16),
            in_specs=[hbm] * 5,
            out_specs=pl.BlockSpec(memory_space=pltpu.VMEM),
            scratch_shapes=[
                vmem((ROWS, HEADS * HD), bf16),
                vmem((ROWS, HD), bf16),
                vmem((ROWS, HD), bf16),
                vmem((1, ROWS), jnp.int32),
                vmem((HEADS * HD, 4 * COLS), bf16),
                vmem((MSG, ROWS), bf16),
                vmem((SLOTS + 2, MSG, ROWS), bf16),
                vmem((HEADS * ROWS, 2 * HD), bf16),
                vmem((2, 2 * HD, 2 * ROWS), bf16),
                vmem((2, 2 * ROWS, 2 * HD), bf16),
                vmem((HEADS * ROWS, 2 * HD), f32),
                vmem((HEADS * ROWS, HD), f32),
                vmem((ROWS, HEADS * HD), bf16),
                vmem((2, ROWS, COLS), f32),
                vmem((2, ROWS, COLS), bf16),
                vmem((2, ROWS, COLS), bf16),
                vmem((ROWS, COLS), bf16),
                vmem((ROWS, COLS), bf16),
                dma((4,)),
                dma((4,)),
                dma((14,)),
                dma((SLOTS + 2,)),
                dma((2, len(CHUNKS))),
                dma((2, len(CHUNKS))),
                dma((len(CHUNKS),)),
                dma((len(CHUNKS),)),
            ],
            compiler_params=pltpu.CompilerParams(
                collective_id=0, has_side_effects=True, vmem_limit_bytes=63 * 2**20),
        )(queries, keys, values, doc_ids.reshape(1, ROWS), w_out)

    placed = (P("ctx", "head"), P("ctx", "head"), P("ctx", "head"), P("ctx"), P("head", None))
    return jax.shard_map(local, mesh=mesh, in_specs=placed, out_specs=P("ctx", "head"), check_vma=False)
```

```python
import functools
import math

import jax
import jax.numpy as jnp
from jax import lax
from jax.experimental import pallas as pl
from jax.experimental.pallas import tpu as pltpu
from jax.sharding import PartitionSpec as P

MESH = pl.DeviceIdType.MESH
HD = 128
ROWS = 256
HEADS = 8
COLS = 640
HIDDEN = -1e30
RATE = math.log2(math.e) / math.sqrt(HD)
CHUNKS = ((0, 64), (64, 64), (128, 128))
KEY_ROWS = HD + 16
MSG = KEY_ROWS + HD
WHOLE, UPPER, LOWER = (0, MSG), (0, KEY_ROWS), (KEY_ROWS, HD)
SLOTS = 8
BEHIND, ROW, LEFT, RIGHT, ROW_LEFT, ROW_RIGHT, ACROSS, ROW_ACROSS = range(SLOTS)
PASS_LEFT, PASS_RIGHT, SPLIT = SLOTS, SLOTS + 1, SLOTS + 2
RING = 4
FAR, NEAR = range(2)
PART = 256


def wide(x, n):
    return jnp.concatenate([x] * n, axis=1)


def kernel(n_ctx, q_hbm, k_hbm, v_hbm, ids_hbm, w_hbm, o_ref,
           q, k, v, marks, w, own, got, rows, kaug, vaug, acc, top, att, keep,
           core_out, core_in, y_out, y_in,
           load_sem, w_sem, send_sem, recv_sem, cs_sem, cr_sem, ys_sem, yr_sem):
    ctx = lax.axis_index("ctx")
    head = lax.axis_index("head")
    y_hi, core = head // 2, lax.rem(head, 2)
    x = lax.rem(ctx, RING)
    base = ctx - x
    inner = (x == 1) | (x == 2)
    right, left = base + lax.rem(x + 1, RING), base + lax.rem(x + RING - 1, RING)
    have_behind, have_row = ctx >= 2 * RING, ctx >= RING
    give_behind, give_row = ctx + 2 * RING < n_ctx, ctx + RING < n_ctx
    mate = y_hi * 2 + (1 - core)
    far = (1 - y_hi) * 2 + core

    barrier = pltpu.get_barrier_semaphore()

    def greet(where, c, h):
        @pl.when(where)
        def _():
            pl.semaphore_signal(barrier, inc=1, device_id=(c, h), device_id_type=MESH)

    greet(have_behind, ctx - 2 * RING, head)
    greet(have_row, ctx - RING, head)
    for c, h in ((left, head), (right, head), (ctx, mate), (ctx, far)):
        greet(True, c, h)

    loads = [pltpu.make_async_copy(src, dst, load_sem.at[i])
             for i, (src, dst) in enumerate([(k_hbm, k), (v_hbm, v), (ids_hbm, marks), (q_hbm, q)])]
    for c in loads:
        c.start()
    for c in loads[:3]:
        c.wait()

    ids = marks[...].astype(jnp.float32)
    own[0:HD, :] = k[...].T
    own[HD:HD + 16, :] = jnp.broadcast_to(ids, (16, ROWS)).astype(jnp.bfloat16)
    own[KEY_ROWS:, 0:HD] = v[0:HD, :]
    own[KEY_ROWS:, HD:] = v[HD:, :]

    greeted = 4 + give_behind.astype(jnp.int32) + give_row.astype(jnp.int32)
    pl.semaphore_wait(barrier, greeted)

    sent = []

    def send(where, src, slot, lane, dest, part=WHOLE, flag=None):
        flag = slot if flag is None else flag
        part = pl.ds(*part)
        copy = pltpu.make_async_remote_copy(
            src_ref=own.at[part] if src is None else got.at[src, part], dst_ref=got.at[slot, part],
            send_sem=send_sem.at[lane], recv_sem=recv_sem.at[flag],
            device_id=(dest, head), device_id_type=MESH)

        @pl.when(where)
        def _():
            copy.start()

        sent.append((where, copy))

    def arrive(slot, where, part=WHOLE, flag=None):
        flag = slot if flag is None else flag
        part = pl.ds(*part)

        @pl.when(where)
        def _():
            pltpu.make_async_remote_copy(
                src_ref=own.at[part], dst_ref=got.at[slot, part], send_sem=send_sem.at[0],
                recv_sem=recv_sem.at[flag], device_id=(left, head), device_id_type=MESH).wait_recv()

    def blank(slot, where):
        @pl.when(where)
        def _():
            got[slot] = jnp.full((MSG, ROWS), -1.0, jnp.bfloat16)

    for slot in (BEHIND, RIGHT, LEFT, ACROSS):
        here = {RIGHT: x < RING - 1, LEFT: x == 0, ACROSS: x < 2}.get(slot, True)
        blank(slot, jnp.logical_not(have_behind) & here)
    for slot in (ROW, ROW_LEFT, ROW_RIGHT, ROW_ACROSS):
        blank(slot, jnp.logical_not(have_row))

    ahead, below = lax.rem(ctx + 2 * RING, n_ctx), lax.rem(ctx + RING, n_ctx)
    send(give_row, None, ROW, 0, below)
    send((x > 0) & give_behind, None, PASS_RIGHT, 1, left)
    send(x < RING - 1, None, LEFT, 2, right)
    send((x == RING - 1) & give_behind, None, PASS_LEFT, 3, right)
    send(x == 0, None, RIGHT, 4, left)

    w_loads = []
    groups = [(1 - y_hi) * 2 + (1 - core), (1 - y_hi) * 2 + core, y_hi * 2 + (1 - core), y_hi * 2 + core]
    for i, g in enumerate(groups):
        c = pltpu.make_async_copy(
            w_hbm.at[:, pl.ds(pl.multiple_of(g * COLS, 128), COLS)], w.at[:, pl.ds(i * COLS, COLS)], w_sem.at[i])
        c.start()
        w_loads.append(c)

    ids_col = jnp.broadcast_to(ids, (HD, ROWS)).T
    first = ids[0:1, 0:1]
    lane = lax.broadcasted_iota(jnp.int32, (ROWS, HD), 1)
    other_doc = jnp.where(ids_col == first, 0.0, 1.0)
    qaug = jnp.where(lane == 0, 1.0, jnp.where(lane == 1, other_doc, 0.0)).astype(jnp.bfloat16)
    t_pos = lax.broadcasted_iota(jnp.int32, (ROWS, ROWS), 0)
    s_pos = lax.broadcasted_iota(jnp.int32, (ROWS, ROWS), 1)
    seen = (wide(ids_col, 2) == ids) & (s_pos <= t_pos)
    dmask = jnp.where(seen, 0.0, HIDDEN)
    kaug[:, HD + 16:, :] = jnp.zeros((2, HD - 16, 2 * ROWS), jnp.bfloat16)
    vaug[:, :, HD:] = jnp.ones((2, 2 * ROWS, HD), jnp.bfloat16)
    vaug[1, 0:HD, 0:HD] = v[0:HD, :]
    vaug[1, HD:ROWS, 0:HD] = v[HD:, :]

    loads[3].wait()
    for t, n in CHUNKS:
        for h in range(HEADS):
            at = t * HEADS + h * n
            rows[at:at + n, 0:HD] = q[t:t + n, h * HD:(h + 1) * HD]
            rows[at:at + n, HD:] = qaug[t:t + n, :]

    for t, n in CHUNKS:
        seen_keys = -(-(t + n) // HD) * HD
        mask = jnp.concatenate([dmask[t:t + n, 0:seen_keys]] * (PART // n), axis=0)
        for at in range(t * HEADS, (t + n) * HEADS, PART):
            here = pl.ds(at, PART)
            s = jnp.dot(rows[here, 0:HD], own[0:HD, 0:seen_keys], preferred_element_type=jnp.float32) + mask
            m = jnp.broadcast_to(jnp.max(s, axis=1, keepdims=True), (PART, HD))
            p = jnp.exp2((s - wide(m, seen_keys // HD)) * RATE).astype(jnp.bfloat16)
            acc[here, :] = jnp.dot(p, vaug[1, 0:seen_keys, :], preferred_element_type=jnp.float32)
            top[here, :] = m

    def fill(slot, b, place):
        cols = pl.ds(place * ROWS, ROWS)
        msg = got.at[slot]
        kaug[b, 0:HD, cols] = msg[0:HD, :]
        bias = jnp.where(msg[HD:HD + 16, :].astype(jnp.float32) == first, 0.0, HIDDEN)
        row = lax.broadcasted_iota(jnp.int32, (16, ROWS), 0)
        kaug[b, HD:HD + 16, cols] = jnp.where(row == 0, bias, jnp.where(row == 1, HIDDEN, 0.0)).astype(jnp.bfloat16)
        vaug[b, place * ROWS:place * ROWS + HD, 0:HD] = msg[KEY_ROWS:, 0:HD]
        vaug[b, place * ROWS + HD:(place + 1) * ROWS, 0:HD] = msg[KEY_ROWS:, HD:]

    def step(here, b, keys):
        s = jnp.dot(rows[here, :], kaug[b, :, keys[0]:keys[1]], preferred_element_type=jnp.float32)
        old = top[here, :]
        m = jnp.maximum(old, jnp.broadcast_to(jnp.max(s, axis=1, keepdims=True), (PART, HD)))
        p = jnp.exp2((s - wide(m, (keys[1] - keys[0]) // HD)) * RATE).astype(jnp.bfloat16)
        shrink = jnp.exp2((old - m) * RATE)
        total = acc[here, :] * wide(shrink, 2) + jnp.dot(p, vaug[b, keys[0]:keys[1], :], preferred_element_type=jnp.float32)
        return m, total

    def fold(b, keys=(0, 2 * ROWS), upto=HEADS * ROWS):
        for at in range(0, upto, PART):
            here = pl.ds(at, PART)
            m, total = step(here, b, keys)
            top[here, :] = m
            acc[here, :] = total

    send(give_behind, None, BEHIND, 5, ahead)
    arrive(ROW, have_row)
    send(have_row, ROW, ROW_LEFT, 8, right)
    send(have_row, ROW, ROW_RIGHT, 9, left)
    arrive(PASS_RIGHT, (x < RING - 1) & give_behind)
    send((x < RING - 1) & give_behind, PASS_RIGHT, RIGHT, 6, ahead)
    arrive(PASS_LEFT, (x == 0) & give_behind)
    send((x == 0) & give_behind, PASS_LEFT, LEFT, 7, ahead)
    arrive(LEFT, x > 0)
    send(inner, LEFT, ACROSS, 10, right)
    arrive(BEHIND, have_behind)
    fill(BEHIND, 0, 0)
    fill(ROW, 0, 1)
    fold(0)
    arrive(ROW_LEFT, have_row)
    send(have_row, ROW_LEFT, ROW_ACROSS, 12, right, UPPER)
    arrive(ROW_RIGHT, have_row)
    send(have_row, ROW_RIGHT, ROW_ACROSS, 13, left, LOWER, SPLIT)
    arrive(RIGHT, inner & have_behind)
    send(inner & have_behind, RIGHT, ACROSS, 11, left)
    arrive(LEFT, (x == 0) & have_behind)
    arrive(RIGHT, (x == RING - 1) | ((x == 0) & have_behind))
    fill(LEFT, 1, 0)
    fill(RIGHT, 1, 1)
    fold(1)
    fill(ROW_LEFT, 0, 0)
    fill(ROW_RIGHT, 0, 1)
    fold(0)
    arrive(ACROSS, have_behind | (x > 1))
    fill(ACROSS, 1, 0)
    arrive(ROW_ACROSS, have_row, UPPER)
    arrive(ROW_ACROSS, have_row, LOWER, SPLIT)
    fill(ROW_ACROSS, 1, 1)

    for c in w_loads:
        c.wait()

    def core_copy(side, c):
        t, n = CHUNKS[c] if side == FAR else (0, ROWS)
        part = pl.ds(t, n)
        return pltpu.make_async_remote_copy(
            src_ref=core_out.at[side, part], dst_ref=core_in.at[side, part], send_sem=cs_sem.at[side, c],
            recv_sem=cr_sem.at[side, c], device_id=(ctx, mate), device_id_type=MESH)

    def y_copy(c):
        t, n = CHUNKS[c]
        part = pl.ds(t, n)
        return pltpu.make_async_remote_copy(
            src_ref=y_out.at[part], dst_ref=y_in.at[part], send_sem=ys_sem.at[c], recv_sem=yr_sem.at[c],
            device_id=(ctx, far), device_id_type=MESH)

    def finish(c):
        t, n = CHUNKS[c]
        for at in range(t * HEADS, (t + n) * HEADS, PART):
            _, total = step(pl.ds(at, PART), 1, (0, 2 * ROWS))
            mean = (total[:, 0:HD] / total[:, HD:]).astype(jnp.bfloat16)
            for i in range(PART // n):
                h = (at - t * HEADS) // n + i
                att[t:t + n, h * HD:(h + 1) * HD] = mean[i * n:(i + 1) * n, :]

    def give(side, c):
        t, n = CHUNKS[c] if side == FAR else (0, ROWS)
        at = 2 * side * COLS
        core_out[side, t:t + n, :] = jnp.dot(
            att[t:t + n, :], w[:, at:at + COLS], preferred_element_type=jnp.float32).astype(jnp.bfloat16)
        core_copy(side, c).start()

    def hold(side, c):
        t, n = CHUNKS[c] if side == FAR else (0, ROWS)
        at = (2 * side + 1) * COLS
        keep[side, t:t + n, :] = jnp.dot(att[t:t + n, :], w[:, at:at + COLS], preferred_element_type=jnp.float32)

    def relay(c):
        t, n = CHUNKS[c]
        core_copy(FAR, c).wait_recv()
        y_out[t:t + n, :] = (keep[FAR, t:t + n, :] + core_in[FAR, t:t + n, :].astype(jnp.float32)).astype(jnp.bfloat16)
        y_copy(c).start()

    finish(0)
    give(FAR, 0)
    hold(FAR, 0)
    finish(1)
    give(FAR, 1)
    hold(FAR, 1)
    relay(0)
    finish(2)
    relay(1)
    give(FAR, 2)
    hold(FAR, 2)
    give(NEAR, 0)
    hold(NEAR, 0)
    relay(2)
    core_copy(NEAR, 0).wait_recv()
    keep[NEAR] += core_in[NEAR].astype(jnp.float32)
    for c, (t, n) in enumerate(CHUNKS):
        y_copy(c).wait_recv()
        o_ref[t:t + n, :] = (keep[NEAR, t:t + n, :] + y_in[t:t + n, :].astype(jnp.float32)).astype(jnp.bfloat16)

    core_copy(NEAR, 0).wait_send()
    for c in range(len(CHUNKS)):
        core_copy(FAR, c).wait_send()
        y_copy(c).wait_send()
    for where, copy in sent:
        @pl.when(where)
        def _():
            copy.wait_send()


def solution(mesh):
    n_ctx = mesh.shape["ctx"]

    def local(queries, keys, values, doc_ids, w_out):
        hbm = pl.BlockSpec(memory_space=pltpu.HBM)
        bf16, f32 = jnp.bfloat16, jnp.float32
        vmem, dma = pltpu.VMEM, pltpu.SemaphoreType.DMA
        return pl.pallas_call(
            functools.partial(kernel, n_ctx),
            out_shape=pltpu.VMEM((ROWS, COLS), bf16),
            in_specs=[hbm] * 5,
            out_specs=pl.BlockSpec(memory_space=pltpu.VMEM),
            scratch_shapes=[
                vmem((ROWS, HEADS * HD), bf16),
                vmem((ROWS, HD), bf16),
                vmem((ROWS, HD), bf16),
                vmem((1, ROWS), jnp.int32),
                vmem((HEADS * HD, 4 * COLS), bf16),
                vmem((MSG, ROWS), bf16),
                vmem((SLOTS + 2, MSG, ROWS), bf16),
                vmem((HEADS * ROWS, 2 * HD), bf16),
                vmem((2, 2 * HD, 2 * ROWS), bf16),
                vmem((2, 2 * ROWS, 2 * HD), bf16),
                vmem((HEADS * ROWS, 2 * HD), f32),
                vmem((HEADS * ROWS, HD), f32),
                vmem((ROWS, HEADS * HD), bf16),
                vmem((2, ROWS, COLS), f32),
                vmem((2, ROWS, COLS), bf16),
                vmem((2, ROWS, COLS), bf16),
                vmem((ROWS, COLS), bf16),
                vmem((ROWS, COLS), bf16),
                dma((4,)),
                dma((4,)),
                dma((14,)),
                dma((SLOTS + 3,)),
                dma((2, len(CHUNKS))),
                dma((2, len(CHUNKS))),
                dma((len(CHUNKS),)),
                dma((len(CHUNKS),)),
            ],
            compiler_params=pltpu.CompilerParams(
                collective_id=0, has_side_effects=True, vmem_limit_bytes=63 * 2**20),
        )(queries, keys, values, doc_ids.reshape(1, ROWS), w_out)

    placed = (P("ctx", "head"), P("ctx", "head"), P("ctx", "head"), P("ctx"), P("head", None))
    return jax.shard_map(local, mesh=mesh, in_specs=placed, out_specs=P("ctx", "head"), check_vma=False)
```

```python
import functools
import math

import jax
import jax.numpy as jnp
from jax import lax
from jax.experimental import pallas as pl
from jax.experimental.pallas import tpu as pltpu
from jax.sharding import PartitionSpec as P

MESH = pl.DeviceIdType.MESH
HD = 128
ROWS = 256
HEADS = 8
COLS = 640
HIDDEN = -1e30
RATE = math.log2(math.e) / math.sqrt(HD)
CHUNKS = ((0, 64), (64, 64), (128, 128))
KEY_ROWS = HD + 16
MSG = KEY_ROWS + HD
WHOLE, UPPER, LOWER = (0, MSG), (0, KEY_ROWS), (KEY_ROWS, HD)
SLOTS = 8
BEHIND, ROW, LEFT, RIGHT, ROW_LEFT, ROW_RIGHT, ACROSS, ROW_ACROSS = range(SLOTS)
PASS_LEFT, PASS_RIGHT, SPLIT = SLOTS, SLOTS + 1, SLOTS + 2
RING = 4
FAR, NEAR = range(2)
PART = 256


def wide(x, n):
    return jnp.concatenate([x] * n, axis=1)


def kernel(n_ctx, q_hbm, k_hbm, v_hbm, ids_hbm, w_hbm, o_ref,
           q, k, v, marks, w, own, got, rows, kaug, vaug, acc, top, att, keep,
           core_out, core_in, y_out, y_in,
           load_sem, w_sem, send_sem, recv_sem, cs_sem, cr_sem, ys_sem, yr_sem):
    ctx = lax.axis_index("ctx")
    head = lax.axis_index("head")
    y_hi, core = head // 2, lax.rem(head, 2)
    x = lax.rem(ctx, RING)
    base = ctx - x
    inner = (x == 1) | (x == 2)
    right, left = base + lax.rem(x + 1, RING), base + lax.rem(x + RING - 1, RING)
    have_behind, have_row = ctx >= 2 * RING, ctx >= RING
    give_behind, give_row = ctx + 2 * RING < n_ctx, ctx + RING < n_ctx
    mate = y_hi * 2 + (1 - core)
    far = (1 - y_hi) * 2 + core

    barrier = pltpu.get_barrier_semaphore()

    def greet(where, c, h):
        @pl.when(where)
        def _():
            pl.semaphore_signal(barrier, inc=1, device_id=(c, h), device_id_type=MESH)

    greet(have_behind, ctx - 2 * RING, head)
    greet(have_row, ctx - RING, head)
    for c, h in ((left, head), (right, head), (ctx, mate), (ctx, far)):
        greet(True, c, h)

    loads = [pltpu.make_async_copy(src, dst, load_sem.at[i])
             for i, (src, dst) in enumerate([(k_hbm, k), (v_hbm, v), (ids_hbm, marks), (q_hbm, q)])]
    for c in loads:
        c.start()
    for c in loads[:3]:
        c.wait()

    ids = marks[...].astype(jnp.float32)
    own[0:HD, :] = k[...].T
    own[HD:HD + 16, :] = jnp.broadcast_to(ids, (16, ROWS)).astype(jnp.bfloat16)
    own[KEY_ROWS:, 0:HD] = v[0:HD, :]
    own[KEY_ROWS:, HD:] = v[HD:, :]

    greeted = 4 + give_behind.astype(jnp.int32) + give_row.astype(jnp.int32)
    pl.semaphore_wait(barrier, greeted)

    sent = []

    def send(where, src, slot, lane, dest, part=WHOLE, flag=None):
        flag = slot if flag is None else flag
        part = pl.ds(*part)
        copy = pltpu.make_async_remote_copy(
            src_ref=own.at[part] if src is None else got.at[src, part], dst_ref=got.at[slot, part],
            send_sem=send_sem.at[lane], recv_sem=recv_sem.at[flag],
            device_id=(dest, head), device_id_type=MESH)

        @pl.when(where)
        def _():
            copy.start()

        sent.append((where, copy))

    def arrive(slot, where, part=WHOLE, flag=None):
        flag = slot if flag is None else flag
        part = pl.ds(*part)

        @pl.when(where)
        def _():
            pltpu.make_async_remote_copy(
                src_ref=own.at[part], dst_ref=got.at[slot, part], send_sem=send_sem.at[0],
                recv_sem=recv_sem.at[flag], device_id=(left, head), device_id_type=MESH).wait_recv()

    def blank(slot, where):
        @pl.when(where)
        def _():
            got[slot] = jnp.full((MSG, ROWS), -1.0, jnp.bfloat16)

    for slot in (BEHIND, RIGHT, LEFT, ACROSS):
        here = {RIGHT: x < RING - 1, LEFT: x == 0, ACROSS: x < 2}.get(slot, True)
        blank(slot, jnp.logical_not(have_behind) & here)
    for slot in (ROW, ROW_LEFT, ROW_RIGHT, ROW_ACROSS):
        blank(slot, jnp.logical_not(have_row))

    ahead, below = lax.rem(ctx + 2 * RING, n_ctx), lax.rem(ctx + RING, n_ctx)
    send(give_row, None, ROW, 0, below)
    send((x > 0) & give_behind, None, PASS_RIGHT, 1, left)
    send(x < RING - 1, None, LEFT, 2, right)
    send((x == RING - 1) & give_behind, None, PASS_LEFT, 3, right)
    send(x == 0, None, RIGHT, 4, left)

    w_loads = []
    groups = [(1 - y_hi) * 2 + (1 - core), (1 - y_hi) * 2 + core, y_hi * 2 + (1 - core), y_hi * 2 + core]
    for i, g in enumerate(groups):
        c = pltpu.make_async_copy(
            w_hbm.at[:, pl.ds(pl.multiple_of(g * COLS, 128), COLS)], w.at[:, pl.ds(i * COLS, COLS)], w_sem.at[i])
        c.start()
        w_loads.append(c)

    ids_col = jnp.broadcast_to(ids, (HD, ROWS)).T
    first = ids[0:1, 0:1]
    lane = lax.broadcasted_iota(jnp.int32, (ROWS, HD), 1)
    other_doc = jnp.where(ids_col == first, 0.0, 1.0)
    qaug = jnp.where(lane == 0, 1.0, jnp.where(lane == 1, other_doc, 0.0)).astype(jnp.bfloat16)
    t_pos = lax.broadcasted_iota(jnp.int32, (ROWS, ROWS), 0)
    s_pos = lax.broadcasted_iota(jnp.int32, (ROWS, ROWS), 1)
    seen = (wide(ids_col, 2) == ids) & (s_pos <= t_pos)
    dmask = jnp.where(seen, 0.0, HIDDEN)
    kaug[:, HD + 16:, :] = jnp.zeros((2, HD - 16, 2 * ROWS), jnp.bfloat16)
    vaug[:, :, HD:] = jnp.ones((2, 2 * ROWS, HD), jnp.bfloat16)
    vaug[1, 0:HD, 0:HD] = v[0:HD, :]
    vaug[1, HD:ROWS, 0:HD] = v[HD:, :]

    loads[3].wait()
    for t, n in CHUNKS:
        for h in range(HEADS):
            at = t * HEADS + h * n
            rows[at:at + n, 0:HD] = q[t:t + n, h * HD:(h + 1) * HD]
            rows[at:at + n, HD:] = qaug[t:t + n, :]

    for t, n in CHUNKS:
        seen_keys = -(-(t + n) // HD) * HD
        mask = jnp.concatenate([dmask[t:t + n, 0:seen_keys]] * (PART // n), axis=0)
        for at in range(t * HEADS, (t + n) * HEADS, PART):
            here = pl.ds(at, PART)
            s = jnp.dot(rows[here, 0:HD], own[0:HD, 0:seen_keys], preferred_element_type=jnp.float32) + mask
            m = jnp.broadcast_to(jnp.max(s, axis=1, keepdims=True), (PART, HD))
            p = jnp.exp2((s - wide(m, seen_keys // HD)) * RATE).astype(jnp.bfloat16)
            acc[here, :] = jnp.dot(p, vaug[1, 0:seen_keys, :], preferred_element_type=jnp.float32)
            top[here, :] = m

    def fill(slot, b, place):
        cols = pl.ds(place * ROWS, ROWS)
        msg = got.at[slot]
        kaug[b, 0:HD, cols] = msg[0:HD, :]
        bias = jnp.where(msg[HD:HD + 16, :].astype(jnp.float32) == first, 0.0, HIDDEN)
        row = lax.broadcasted_iota(jnp.int32, (16, ROWS), 0)
        kaug[b, HD:HD + 16, cols] = jnp.where(row == 0, bias, jnp.where(row == 1, HIDDEN, 0.0)).astype(jnp.bfloat16)
        vaug[b, place * ROWS:place * ROWS + HD, 0:HD] = msg[KEY_ROWS:, 0:HD]
        vaug[b, place * ROWS + HD:(place + 1) * ROWS, 0:HD] = msg[KEY_ROWS:, HD:]

    def step(here, b, keys):
        s = jnp.dot(rows[here, :], kaug[b, :, keys[0]:keys[1]], preferred_element_type=jnp.float32)
        old = top[here, :]
        m = jnp.maximum(old, jnp.broadcast_to(jnp.max(s, axis=1, keepdims=True), (PART, HD)))
        p = jnp.exp2((s - wide(m, (keys[1] - keys[0]) // HD)) * RATE).astype(jnp.bfloat16)
        shrink = jnp.exp2((old - m) * RATE)
        total = acc[here, :] * wide(shrink, 2) + jnp.dot(p, vaug[b, keys[0]:keys[1], :], preferred_element_type=jnp.float32)
        return m, total

    def fold(b, keys=(0, 2 * ROWS), upto=HEADS * ROWS):
        for at in range(0, upto, PART):
            here = pl.ds(at, PART)
            m, total = step(here, b, keys)
            top[here, :] = m
            acc[here, :] = total

    send(give_behind, None, BEHIND, 5, ahead)
    arrive(ROW, have_row)
    send(have_row, ROW, ROW_LEFT, 8, right)
    send(have_row, ROW, ROW_RIGHT, 9, left)
    arrive(PASS_RIGHT, (x < RING - 1) & give_behind)
    send((x < RING - 1) & give_behind, PASS_RIGHT, RIGHT, 6, ahead)
    arrive(PASS_LEFT, (x == 0) & give_behind)
    send((x == 0) & give_behind, PASS_LEFT, LEFT, 7, ahead)
    arrive(LEFT, x > 0)
    send(inner, LEFT, ACROSS, 10, right)
    arrive(BEHIND, have_behind)
    fill(BEHIND, 0, 0)
    fill(ROW, 0, 1)
    fold(0)
    arrive(RIGHT, inner & have_behind)
    send(inner & have_behind, RIGHT, ACROSS, 11, left)
    arrive(ROW_LEFT, have_row)
    send(have_row, ROW_LEFT, ROW_ACROSS, 12, right, UPPER)
    arrive(ROW_RIGHT, have_row)
    send(have_row, ROW_RIGHT, ROW_ACROSS, 13, left, LOWER, SPLIT)
    arrive(LEFT, (x == 0) & have_behind)
    arrive(RIGHT, (x == RING - 1) | ((x == 0) & have_behind))
    fill(LEFT, 1, 0)
    fill(RIGHT, 1, 1)
    fold(1)
    fill(ROW_LEFT, 0, 0)
    fill(ROW_RIGHT, 0, 1)
    fold(0)
    arrive(ACROSS, have_behind | (x > 1))
    fill(ACROSS, 1, 0)
    arrive(ROW_ACROSS, have_row, UPPER)
    arrive(ROW_ACROSS, have_row, LOWER, SPLIT)
    fill(ROW_ACROSS, 1, 1)

    for c in w_loads:
        c.wait()

    def core_copy(side, c):
        t, n = CHUNKS[c] if side == FAR else (0, ROWS)
        part = pl.ds(t, n)
        return pltpu.make_async_remote_copy(
            src_ref=core_out.at[side, part], dst_ref=core_in.at[side, part], send_sem=cs_sem.at[side, c],
            recv_sem=cr_sem.at[side, c], device_id=(ctx, mate), device_id_type=MESH)

    def y_copy(c):
        t, n = CHUNKS[c]
        part = pl.ds(t, n)
        return pltpu.make_async_remote_copy(
            src_ref=y_out.at[part], dst_ref=y_in.at[part], send_sem=ys_sem.at[c], recv_sem=yr_sem.at[c],
            device_id=(ctx, far), device_id_type=MESH)

    def finish(c):
        t, n = CHUNKS[c]
        for at in range(t * HEADS, (t + n) * HEADS, PART):
            _, total = step(pl.ds(at, PART), 1, (0, 2 * ROWS))
            mean = (total[:, 0:HD] / total[:, HD:]).astype(jnp.bfloat16)
            for i in range(PART // n):
                h = (at - t * HEADS) // n + i
                att[t:t + n, h * HD:(h + 1) * HD] = mean[i * n:(i + 1) * n, :]

    def give(side, c):
        t, n = CHUNKS[c] if side == FAR else (0, ROWS)
        at = 2 * side * COLS
        core_out[side, t:t + n, :] = jnp.dot(
            att[t:t + n, :], w[:, at:at + COLS], preferred_element_type=jnp.float32).astype(jnp.bfloat16)
        core_copy(side, c).start()

    def hold(side, c):
        t, n = CHUNKS[c] if side == FAR else (0, ROWS)
        at = (2 * side + 1) * COLS
        keep[side, t:t + n, :] = jnp.dot(att[t:t + n, :], w[:, at:at + COLS], preferred_element_type=jnp.float32)

    def relay(c):
        t, n = CHUNKS[c]
        core_copy(FAR, c).wait_recv()
        y_out[t:t + n, :] = (keep[FAR, t:t + n, :] + core_in[FAR, t:t + n, :].astype(jnp.float32)).astype(jnp.bfloat16)
        y_copy(c).start()

    finish(0)
    give(FAR, 0)
    hold(FAR, 0)
    finish(1)
    give(FAR, 1)
    hold(FAR, 1)
    relay(0)
    finish(2)
    relay(1)
    give(FAR, 2)
    hold(FAR, 2)
    give(NEAR, 0)
    hold(NEAR, 0)
    relay(2)
    core_copy(NEAR, 0).wait_recv()
    keep[NEAR] += core_in[NEAR].astype(jnp.float32)
    for c, (t, n) in enumerate(CHUNKS):
        y_copy(c).wait_recv()
        o_ref[t:t + n, :] = (keep[NEAR, t:t + n, :] + y_in[t:t + n, :].astype(jnp.float32)).astype(jnp.bfloat16)

    core_copy(NEAR, 0).wait_send()
    for c in range(len(CHUNKS)):
        core_copy(FAR, c).wait_send()
        y_copy(c).wait_send()
    for where, copy in sent:
        @pl.when(where)
        def _():
            copy.wait_send()


def solution(mesh):
    n_ctx = mesh.shape["ctx"]

    def local(queries, keys, values, doc_ids, w_out):
        hbm = pl.BlockSpec(memory_space=pltpu.HBM)
        bf16, f32 = jnp.bfloat16, jnp.float32
        vmem, dma = pltpu.VMEM, pltpu.SemaphoreType.DMA
        return pl.pallas_call(
            functools.partial(kernel, n_ctx),
            out_shape=pltpu.VMEM((ROWS, COLS), bf16),
            in_specs=[hbm] * 5,
            out_specs=pl.BlockSpec(memory_space=pltpu.VMEM),
            scratch_shapes=[
                vmem((ROWS, HEADS * HD), bf16),
                vmem((ROWS, HD), bf16),
                vmem((ROWS, HD), bf16),
                vmem((1, ROWS), jnp.int32),
                vmem((HEADS * HD, 4 * COLS), bf16),
                vmem((MSG, ROWS), bf16),
                vmem((SLOTS + 2, MSG, ROWS), bf16),
                vmem((HEADS * ROWS, 2 * HD), bf16),
                vmem((2, 2 * HD, 2 * ROWS), bf16),
                vmem((2, 2 * ROWS, 2 * HD), bf16),
                vmem((HEADS * ROWS, 2 * HD), f32),
                vmem((HEADS * ROWS, HD), f32),
                vmem((ROWS, HEADS * HD), bf16),
                vmem((2, ROWS, COLS), f32),
                vmem((2, ROWS, COLS), bf16),
                vmem((2, ROWS, COLS), bf16),
                vmem((ROWS, COLS), bf16),
                vmem((ROWS, COLS), bf16),
                dma((4,)),
                dma((4,)),
                dma((14,)),
                dma((SLOTS + 3,)),
                dma((2, len(CHUNKS))),
                dma((2, len(CHUNKS))),
                dma((len(CHUNKS),)),
                dma((len(CHUNKS),)),
            ],
            compiler_params=pltpu.CompilerParams(
                collective_id=0, has_side_effects=True, vmem_limit_bytes=63 * 2**20),
        )(queries, keys, values, doc_ids.reshape(1, ROWS), w_out)

    placed = (P("ctx", "head"), P("ctx", "head"), P("ctx", "head"), P("ctx"), P("head", None))
    return jax.shard_map(local, mesh=mesh, in_specs=placed, out_specs=P("ctx", "head"), check_vma=False)
```

```python
import functools
import math

import jax
import jax.numpy as jnp
from jax import lax
from jax.experimental import pallas as pl
from jax.experimental.pallas import tpu as pltpu
from jax.sharding import PartitionSpec as P

MESH = pl.DeviceIdType.MESH
HD = 128
ROWS = 256
HEADS = 8
COLS = 640
HIDDEN = -1e30
RATE = math.log2(math.e) / math.sqrt(HD)
CHUNKS = ((0, 64), (64, 64), (128, 128))
KEY_ROWS = HD + 16
MSG = KEY_ROWS + HD
WHOLE, UPPER, LOWER = (0, MSG), (0, KEY_ROWS), (KEY_ROWS, HD)
SLOTS = 8
BEHIND, ROW, LEFT, RIGHT, ROW_LEFT, ROW_RIGHT, ACROSS, ROW_ACROSS = range(SLOTS)
PASS_LEFT, PASS_RIGHT, SPLIT = SLOTS, SLOTS + 1, SLOTS + 2
RING = 4
FAR, NEAR = range(2)
PART = 256


def wide(x, n):
    return jnp.concatenate([x] * n, axis=1)


def kernel(n_ctx, q_hbm, k_hbm, v_hbm, ids_hbm, w_hbm, o_ref,
           q, k, v, marks, w, own, got, rows, kaug, vaug, acc, top, att, keep,
           core_out, core_in, y_out, y_in,
           load_sem, w_sem, send_sem, recv_sem, cs_sem, cr_sem, ys_sem, yr_sem):
    ctx = lax.axis_index("ctx")
    head = lax.axis_index("head")
    y_hi, core = head // 2, lax.rem(head, 2)
    x = lax.rem(ctx, RING)
    base = ctx - x
    inner = (x == 1) | (x == 2)
    right, left = base + lax.rem(x + 1, RING), base + lax.rem(x + RING - 1, RING)
    have_behind, have_row = ctx >= 2 * RING, ctx >= RING
    give_behind, give_row = ctx + 2 * RING < n_ctx, ctx + RING < n_ctx
    mate = y_hi * 2 + (1 - core)
    far = (1 - y_hi) * 2 + core

    barrier = pltpu.get_barrier_semaphore()

    def greet(where, c, h):
        @pl.when(where)
        def _():
            pl.semaphore_signal(barrier, inc=1, device_id=(c, h), device_id_type=MESH)

    greet(have_behind, ctx - 2 * RING, head)
    greet(have_row, ctx - RING, head)
    for c, h in ((left, head), (right, head), (ctx, mate), (ctx, far)):
        greet(True, c, h)

    loads = [pltpu.make_async_copy(src, dst, load_sem.at[i])
             for i, (src, dst) in enumerate([(k_hbm, k), (v_hbm, v), (ids_hbm, marks), (q_hbm, q)])]
    for c in loads:
        c.start()
    for c in loads[:3]:
        c.wait()

    ids = marks[...].astype(jnp.float32)
    own[0:HD, :] = k[...].T
    own[HD:HD + 16, :] = jnp.broadcast_to(ids, (16, ROWS)).astype(jnp.bfloat16)
    own[KEY_ROWS:, 0:HD] = v[0:HD, :]
    own[KEY_ROWS:, HD:] = v[HD:, :]

    greeted = 4 + give_behind.astype(jnp.int32) + give_row.astype(jnp.int32)
    pl.semaphore_wait(barrier, greeted)

    sent = []

    def send(where, src, slot, lane, dest, part=WHOLE, flag=None):
        flag = slot if flag is None else flag
        part = pl.ds(*part)
        copy = pltpu.make_async_remote_copy(
            src_ref=own.at[part] if src is None else got.at[src, part], dst_ref=got.at[slot, part],
            send_sem=send_sem.at[lane], recv_sem=recv_sem.at[flag],
            device_id=(dest, head), device_id_type=MESH)

        @pl.when(where)
        def _():
            copy.start()

        sent.append((where, copy))

    def arrive(slot, where, part=WHOLE, flag=None):
        flag = slot if flag is None else flag
        part = pl.ds(*part)

        @pl.when(where)
        def _():
            pltpu.make_async_remote_copy(
                src_ref=own.at[part], dst_ref=got.at[slot, part], send_sem=send_sem.at[0],
                recv_sem=recv_sem.at[flag], device_id=(left, head), device_id_type=MESH).wait_recv()

    def blank(slot, where):
        @pl.when(where)
        def _():
            got[slot] = jnp.full((MSG, ROWS), -1.0, jnp.bfloat16)

    for slot in (BEHIND, RIGHT, LEFT, ACROSS):
        here = {RIGHT: x < RING - 1, LEFT: x == 0, ACROSS: x < 2}.get(slot, True)
        blank(slot, jnp.logical_not(have_behind) & here)
    for slot in (ROW, ROW_LEFT, ROW_RIGHT, ROW_ACROSS):
        blank(slot, jnp.logical_not(have_row))

    ahead, below = lax.rem(ctx + 2 * RING, n_ctx), lax.rem(ctx + RING, n_ctx)
    send(give_row, None, ROW, 0, below)
    send((x > 0) & give_behind, None, PASS_RIGHT, 1, left)
    send(x < RING - 1, None, LEFT, 2, right)
    send((x == RING - 1) & give_behind, None, PASS_LEFT, 3, right)
    send(x == 0, None, RIGHT, 4, left)

    send(give_behind & (lax.rem(ctx // RING, 2) == 1), None, BEHIND, 5, ahead)
    w_loads = []
    groups = [(1 - y_hi) * 2 + (1 - core), (1 - y_hi) * 2 + core, y_hi * 2 + (1 - core), y_hi * 2 + core]
    for i, g in enumerate(groups):
        c = pltpu.make_async_copy(
            w_hbm.at[:, pl.ds(pl.multiple_of(g * COLS, 128), COLS)], w.at[:, pl.ds(i * COLS, COLS)], w_sem.at[i])
        c.start()
        w_loads.append(c)

    ids_col = jnp.broadcast_to(ids, (HD, ROWS)).T
    first = ids[0:1, 0:1]
    lane = lax.broadcasted_iota(jnp.int32, (ROWS, HD), 1)
    other_doc = jnp.where(ids_col == first, 0.0, 1.0)
    qaug = jnp.where(lane == 0, 1.0, jnp.where(lane == 1, other_doc, 0.0)).astype(jnp.bfloat16)
    t_pos = lax.broadcasted_iota(jnp.int32, (ROWS, ROWS), 0)
    s_pos = lax.broadcasted_iota(jnp.int32, (ROWS, ROWS), 1)
    seen = (wide(ids_col, 2) == ids) & (s_pos <= t_pos)
    dmask = jnp.where(seen, 0.0, HIDDEN)
    kaug[:, HD + 16:, :] = jnp.zeros((2, HD - 16, 2 * ROWS), jnp.bfloat16)
    vaug[:, :, HD:] = jnp.ones((2, 2 * ROWS, HD), jnp.bfloat16)
    vaug[1, 0:HD, 0:HD] = v[0:HD, :]
    vaug[1, HD:ROWS, 0:HD] = v[HD:, :]

    loads[3].wait()
    for t, n in CHUNKS:
        for h in range(HEADS):
            at = t * HEADS + h * n
            rows[at:at + n, 0:HD] = q[t:t + n, h * HD:(h + 1) * HD]
            rows[at:at + n, HD:] = qaug[t:t + n, :]

    for t, n in CHUNKS:
        seen_keys = -(-(t + n) // HD) * HD
        mask = jnp.concatenate([dmask[t:t + n, 0:seen_keys]] * (PART // n), axis=0)
        for at in range(t * HEADS, (t + n) * HEADS, PART):
            here = pl.ds(at, PART)
            s = jnp.dot(rows[here, 0:HD], own[0:HD, 0:seen_keys], preferred_element_type=jnp.float32) + mask
            m = jnp.broadcast_to(jnp.max(s, axis=1, keepdims=True), (PART, HD))
            p = jnp.exp2((s - wide(m, seen_keys // HD)) * RATE).astype(jnp.bfloat16)
            acc[here, :] = jnp.dot(p, vaug[1, 0:seen_keys, :], preferred_element_type=jnp.float32)
            top[here, :] = m

    def fill(slot, b, place):
        cols = pl.ds(place * ROWS, ROWS)
        msg = got.at[slot]
        kaug[b, 0:HD, cols] = msg[0:HD, :]
        bias = jnp.where(msg[HD:HD + 16, :].astype(jnp.float32) == first, 0.0, HIDDEN)
        row = lax.broadcasted_iota(jnp.int32, (16, ROWS), 0)
        kaug[b, HD:HD + 16, cols] = jnp.where(row == 0, bias, jnp.where(row == 1, HIDDEN, 0.0)).astype(jnp.bfloat16)
        vaug[b, place * ROWS:place * ROWS + HD, 0:HD] = msg[KEY_ROWS:, 0:HD]
        vaug[b, place * ROWS + HD:(place + 1) * ROWS, 0:HD] = msg[KEY_ROWS:, HD:]

    def step(here, b, keys):
        s = jnp.dot(rows[here, :], kaug[b, :, keys[0]:keys[1]], preferred_element_type=jnp.float32)
        old = top[here, :]
        m = jnp.maximum(old, jnp.broadcast_to(jnp.max(s, axis=1, keepdims=True), (PART, HD)))
        p = jnp.exp2((s - wide(m, (keys[1] - keys[0]) // HD)) * RATE).astype(jnp.bfloat16)
        shrink = jnp.exp2((old - m) * RATE)
        total = acc[here, :] * wide(shrink, 2) + jnp.dot(p, vaug[b, keys[0]:keys[1], :], preferred_element_type=jnp.float32)
        return m, total

    def fold(b, keys=(0, 2 * ROWS), upto=HEADS * ROWS):
        for at in range(0, upto, PART):
            here = pl.ds(at, PART)
            m, total = step(here, b, keys)
            top[here, :] = m
            acc[here, :] = total

    send(give_behind & (lax.rem(ctx // RING, 2) == 0), None, BEHIND, 5, ahead)
    arrive(ROW, have_row)
    send(have_row, ROW, ROW_LEFT, 8, right)
    send(have_row, ROW, ROW_RIGHT, 9, left)
    arrive(PASS_RIGHT, (x < RING - 1) & give_behind)
    send((x < RING - 1) & give_behind, PASS_RIGHT, RIGHT, 6, ahead)
    arrive(PASS_LEFT, (x == 0) & give_behind)
    send((x == 0) & give_behind, PASS_LEFT, LEFT, 7, ahead)
    arrive(LEFT, x > 0)
    send(inner, LEFT, ACROSS, 10, right)
    arrive(BEHIND, have_behind)
    fill(BEHIND, 0, 0)
    fill(ROW, 0, 1)
    fold(0)
    arrive(RIGHT, inner & have_behind)
    send(inner & have_behind, RIGHT, ACROSS, 11, left)
    arrive(ROW_LEFT, have_row)
    send(have_row, ROW_LEFT, ROW_ACROSS, 12, right, UPPER)
    arrive(ROW_RIGHT, have_row)
    send(have_row, ROW_RIGHT, ROW_ACROSS, 13, left, LOWER, SPLIT)
    arrive(LEFT, (x == 0) & have_behind)
    arrive(RIGHT, (x == RING - 1) | ((x == 0) & have_behind))
    fill(LEFT, 1, 0)
    fill(RIGHT, 1, 1)
    fold(1)
    fill(ROW_LEFT, 0, 0)
    fill(ROW_RIGHT, 0, 1)
    fold(0)
    arrive(ACROSS, have_behind | (x > 1))
    fill(ACROSS, 1, 0)
    arrive(ROW_ACROSS, have_row, UPPER)
    arrive(ROW_ACROSS, have_row, LOWER, SPLIT)
    fill(ROW_ACROSS, 1, 1)

    for c in w_loads:
        c.wait()

    def core_copy(side, c):
        t, n = CHUNKS[c] if side == FAR else (0, ROWS)
        part = pl.ds(t, n)
        return pltpu.make_async_remote_copy(
            src_ref=core_out.at[side, part], dst_ref=core_in.at[side, part], send_sem=cs_sem.at[side, c],
            recv_sem=cr_sem.at[side, c], device_id=(ctx, mate), device_id_type=MESH)

    def y_copy(c):
        t, n = CHUNKS[c]
        part = pl.ds(t, n)
        return pltpu.make_async_remote_copy(
            src_ref=y_out.at[part], dst_ref=y_in.at[part], send_sem=ys_sem.at[c], recv_sem=yr_sem.at[c],
            device_id=(ctx, far), device_id_type=MESH)

    def finish(c):
        t, n = CHUNKS[c]
        for at in range(t * HEADS, (t + n) * HEADS, PART):
            _, total = step(pl.ds(at, PART), 1, (0, 2 * ROWS))
            mean = (total[:, 0:HD] / total[:, HD:]).astype(jnp.bfloat16)
            for i in range(PART // n):
                h = (at - t * HEADS) // n + i
                att[t:t + n, h * HD:(h + 1) * HD] = mean[i * n:(i + 1) * n, :]

    def give(side, c):
        t, n = CHUNKS[c] if side == FAR else (0, ROWS)
        at = 2 * side * COLS
        core_out[side, t:t + n, :] = jnp.dot(
            att[t:t + n, :], w[:, at:at + COLS], preferred_element_type=jnp.float32).astype(jnp.bfloat16)
        core_copy(side, c).start()

    def hold(side, c):
        t, n = CHUNKS[c] if side == FAR else (0, ROWS)
        at = (2 * side + 1) * COLS
        keep[side, t:t + n, :] = jnp.dot(att[t:t + n, :], w[:, at:at + COLS], preferred_element_type=jnp.float32)

    def relay(c):
        t, n = CHUNKS[c]
        core_copy(FAR, c).wait_recv()
        y_out[t:t + n, :] = (keep[FAR, t:t + n, :] + core_in[FAR, t:t + n, :].astype(jnp.float32)).astype(jnp.bfloat16)
        y_copy(c).start()

    finish(0)
    give(FAR, 0)
    hold(FAR, 0)
    finish(1)
    give(FAR, 1)
    hold(FAR, 1)
    relay(0)
    finish(2)
    relay(1)
    give(FAR, 2)
    hold(FAR, 2)
    give(NEAR, 0)
    hold(NEAR, 0)
    relay(2)
    core_copy(NEAR, 0).wait_recv()
    keep[NEAR] += core_in[NEAR].astype(jnp.float32)
    for c, (t, n) in enumerate(CHUNKS):
        y_copy(c).wait_recv()
        o_ref[t:t + n, :] = (keep[NEAR, t:t + n, :] + y_in[t:t + n, :].astype(jnp.float32)).astype(jnp.bfloat16)

    core_copy(NEAR, 0).wait_send()
    for c in range(len(CHUNKS)):
        core_copy(FAR, c).wait_send()
        y_copy(c).wait_send()
    for where, copy in sent:
        @pl.when(where)
        def _():
            copy.wait_send()


def solution(mesh):
    n_ctx = mesh.shape["ctx"]

    def local(queries, keys, values, doc_ids, w_out):
        hbm = pl.BlockSpec(memory_space=pltpu.HBM)
        bf16, f32 = jnp.bfloat16, jnp.float32
        vmem, dma = pltpu.VMEM, pltpu.SemaphoreType.DMA
        return pl.pallas_call(
            functools.partial(kernel, n_ctx),
            out_shape=pltpu.VMEM((ROWS, COLS), bf16),
            in_specs=[hbm] * 5,
            out_specs=pl.BlockSpec(memory_space=pltpu.VMEM),
            scratch_shapes=[
                vmem((ROWS, HEADS * HD), bf16),
                vmem((ROWS, HD), bf16),
                vmem((ROWS, HD), bf16),
                vmem((1, ROWS), jnp.int32),
                vmem((HEADS * HD, 4 * COLS), bf16),
                vmem((MSG, ROWS), bf16),
                vmem((SLOTS + 2, MSG, ROWS), bf16),
                vmem((HEADS * ROWS, 2 * HD), bf16),
                vmem((2, 2 * HD, 2 * ROWS), bf16),
                vmem((2, 2 * ROWS, 2 * HD), bf16),
                vmem((HEADS * ROWS, 2 * HD), f32),
                vmem((HEADS * ROWS, HD), f32),
                vmem((ROWS, HEADS * HD), bf16),
                vmem((2, ROWS, COLS), f32),
                vmem((2, ROWS, COLS), bf16),
                vmem((2, ROWS, COLS), bf16),
                vmem((ROWS, COLS), bf16),
                vmem((ROWS, COLS), bf16),
                dma((4,)),
                dma((4,)),
                dma((14,)),
                dma((SLOTS + 3,)),
                dma((2, len(CHUNKS))),
                dma((2, len(CHUNKS))),
                dma((len(CHUNKS),)),
                dma((len(CHUNKS),)),
            ],
            compiler_params=pltpu.CompilerParams(
                collective_id=0, has_side_effects=True, vmem_limit_bytes=63 * 2**20),
        )(queries, keys, values, doc_ids.reshape(1, ROWS), w_out)

    placed = (P("ctx", "head"), P("ctx", "head"), P("ctx", "head"), P("ctx"), P("head", None))
    return jax.shard_map(local, mesh=mesh, in_specs=placed, out_specs=P("ctx", "head"), check_vma=False)
```
